128 devices in a mesh: row: 8 (over x_hi, y), col: 16 (over x_lo, z, core).
Axes of the slice: x: 4 (x_hi: 2, x_lo: 2; x = x_hi * 2 + x_lo), y: 4, z: 4, core: 2. Of those that a mesh axis runs over, the one named last changes fastest.
Arguments:
- atom_feat: bfloat16 [32768, 128], P(('row', 'col')), may hold values from -6 to 6
- atom_token: int32 [32768], P(('row', 'col')), may hold values from 0 to 2047, as said below
- atom_count: int32 [128], P(('row', 'col')), may hold values from 128 to 256
- window_start: int32 [1024], P(('row', 'col')), may hold values from -64 to 192, as said below
- w_atom_qkv: bfloat16 [128, 384], replicated, may hold values from -2 to 2
- w_atom_out: bfloat16 [128, 128], replicated, may hold values from -0.5 to 0.5
- w_atom_tok: bfloat16 [128, 768], replicated, may hold values from -0.5 to 0.5
- single: bfloat16 [2048, 768], P(('row', 'col')), may hold values from -6 to 6
- tok_gain: float32 [768], replicated, may hold values from 0.1 to 1.9
- w_tok: bfloat16 [768, 3072], replicated, may hold values from -3 to 3
- w_tok_out: bfloat16 [768, 768], replicated, may hold values from -0.21875 to 0.21875
- pair: bfloat16 [2048, 2048, 128], P('row', 'col'), may hold values from -6 to 6
- w_pair_in: bfloat16 [128, 512], replicated, may hold values from -0.5 to 0.5
- w_pair_out: bfloat16 [256, 128], replicated, may hold values from -0.375 to 0.375
- w_bias: bfloat16 [128, 16], replicated, may hold values from -1.5 to 1.5
- w_back: bfloat16 [768, 128], replicated, may hold values from -0.21875 to 0.21875
Outputs:
- token_out: bfloat16 [2048, 768], P(('row', 'col'))
- atom_out: bfloat16 [32768, 128], P(('row', 'col'))
- pair_out: bfloat16 [2048, 2048, 128], P('row', 'col')
The draws below stay inside these ranges and needn't reach their ends.
Inputs may be any that keep to these rules, and one draw needn't show every extreme that they name: `atom_token`: block d of 256 slots holds only tokens d * 16 to d * 16 + 15; over its first atom_count[d] slots the values never fall and name every token of the block; the other slots name the block's last token. `window_start`: window b of a block starts between 32 b - 64 and 32 b - 32.
All inputs are finite; a program needn't handle non-finite values.
Results may differ from the reference program's by a relative error of at most 0.008.
The reference program's roundings to bfloat16 on the way count: a program that leaves them out, or rounds other values in their place, can miss the bound.
Values may be sent and summed in bfloat16 or wider, within the bound.
A program may use at most 128 MiB of HBM per device.

```python
import math
from functools import partial
import jax
import jax.numpy as jnp
from jax import lax

C_ATOM = 128
ATOM_HEADS = 4
C_TOK = 768
TOK_HEADS = 16
C_PAIR = 128
PAIR_HID = 256
QUERY_BLOCK = 32
KEY_WINDOW = 128
TOK_DEV = 16
ATOM_CAP = 256
TOKENS = 2048
ATOMS = 32768


def shared_counts(key):
    key = jax.random.fold_in(key, 11)
    blocks_total = ATOMS // ATOM_CAP
    key_count, key_order = jax.random.split(key)
    counts = jax.random.randint(key_count, (blocks_total,), ATOM_CAP // 2, ATOM_CAP + 1)
    permuted = jax.random.permutation(key_order, blocks_total)
    counts = counts.at[permuted[0]].set(ATOM_CAP).at[permuted[1]].set(ATOM_CAP // 2)
    return counts.astype(jnp.int32)


def draw_atom_count(key, part):
    counts = shared_counts(key)
    return counts


def draw_atom_token(key, part):
    counts = shared_counts(key)
    key = jax.random.fold_in(key, 5)
    blocks_total = ATOMS // ATOM_CAP
    raw_tokens = jax.random.randint(key, (blocks_total, ATOM_CAP), 0, TOK_DEV)
    slot_ids = jnp.arange(ATOM_CAP, dtype=jnp.int32)
    raw_tokens = jnp.where(slot_ids[None, :] < TOK_DEV, slot_ids[None, :], raw_tokens)
    live_slot = slot_ids[None, :] < counts[:, None]
    ordered = jnp.sort(jnp.where(live_slot, raw_tokens, TOK_DEV), axis=1)
    local_tokens = jnp.minimum(ordered, TOK_DEV - 1)
    block_base = jnp.arange(blocks_total, dtype=jnp.int32)[:, None] * TOK_DEV
    return (local_tokens + block_base).reshape(-1).astype(jnp.int32)


def draw_window_start(key, part):
    key = jax.random.fold_in(key, 7)
    blocks_total = ATOMS // ATOM_CAP
    windows_each = ATOM_CAP // QUERY_BLOCK
    jitter = jax.random.randint(key, (blocks_total, windows_each), 0, KEY_WINDOW // 2 - QUERY_BLOCK + 1)
    jitter = jitter.at[0, 0].set(0).at[blocks_total - 1, windows_each - 1].set(KEY_WINDOW // 2 - QUERY_BLOCK)
    window_base = jnp.arange(windows_each, dtype=jnp.int32) * QUERY_BLOCK - KEY_WINDOW // 2
    return (window_base[None, :] + jitter).reshape(-1).astype(jnp.int32)


def normal_block(key, shape):
    return jnp.clip(jax.random.normal(key, shape, jnp.float32), -6.0, 6.0)


def draw_w_atom_qkv(key, part):
    key = jax.random.fold_in(key, 13)
    key_query = jax.random.fold_in(key, 1)
    key_key = jax.random.fold_in(key, 2)
    key_value = jax.random.fold_in(key, 3)
    shape = (C_ATOM, C_ATOM)
    queries = normal_block(key_query, shape)
    keys = normal_block(key_key, shape)
    values = normal_block(key_value, shape)
    return (0.15 * jnp.concatenate([queries, keys, values], axis=1)).astype(jnp.bfloat16)


def draw_w_tok(key, part):
    key = jax.random.fold_in(key, 17)
    key_query = jax.random.fold_in(key, 1)
    key_key = jax.random.fold_in(key, 2)
    key_rest = jax.random.fold_in(key, 3)
    scale = C_TOK ** (-0.5)
    queries = normal_block(key_query, (C_TOK, C_TOK))
    keys = normal_block(key_key, (C_TOK, C_TOK))
    rest = normal_block(key_rest, (C_TOK, 2 * C_TOK))
    return (scale * jnp.concatenate([queries, keys, rest], axis=1)).astype(jnp.bfloat16)


def level_of(key, dims, cuts, low, top_value):
    def one(dim, shards_of):
        heights = jax.random.uniform(jax.random.fold_in(jax.random.fold_in(key, 6), dim), (shards_of,), jnp.float32, low / len(cuts), top_value / len(cuts))
        return jnp.repeat(jnp.exp(heights), dims[dim] // shards_of).reshape((-1,) + (1,) * (len(dims) - dim - 1))

    factor_of = one(*cuts[0])
    for cut in cuts[1:]:
        factor_of = factor_of * one(*cut)
    return factor_of


def scatter_about(rng, dims, scale, limit, cuts=(), kind=jnp.bfloat16):
    array = jax.random.normal(rng, dims, jnp.float32) * scale
    if len(cuts) > 0:
        array = level_of(rng, dims, cuts, -0.22, 0.18) * array
    return jnp.clip(array, min=-limit, max=limit).astype(kind)


def setup_inputs(seed: int = 0) -> dict:
    key_list = jax.random.split(jax.random.key(seed), 17)
    atom_feat = scatter_about(key_list[0], (ATOMS, C_ATOM), 1.0, 6.0, ((0, 128),))
    atom_token = draw_atom_token(jax.random.fold_in(key_list[16], 71), 0)
    atom_count = draw_atom_count(jax.random.fold_in(key_list[16], 71), 0)
    window_start = draw_window_start(jax.random.fold_in(key_list[16], 71), 0)
    w_atom_qkv = draw_w_atom_qkv(jax.random.fold_in(key_list[16], 71), 0)
    w_atom_out = scatter_about(key_list[5], (C_ATOM, C_ATOM), C_ATOM ** -0.5, 0.5)
    w_atom_tok = scatter_about(key_list[6], (C_ATOM, C_TOK), C_ATOM ** -0.5, 0.5)
    single = scatter_about(key_list[7], (TOKENS, C_TOK), 1.0, 6.0, ((0, 128),))
    tok_gain = jnp.clip(1.0 + 0.18 * jax.random.normal(key_list[8], (C_TOK,), jnp.float32), 0.1, 1.9)
    w_tok = draw_w_tok(jax.random.fold_in(key_list[16], 71), 0)
    w_tok_out = scatter_about(key_list[10], (C_TOK, C_TOK), C_TOK ** -0.5, 0.21875)
    pair = scatter_about(key_list[11], (TOKENS, TOKENS, C_PAIR), 1.0, 6.0, ((0, 8), (1, 16)))
    w_pair_in = scatter_about(key_list[12], (C_PAIR, 2 * PAIR_HID), C_PAIR ** -0.5, 0.5)
    w_pair_out = scatter_about(key_list[13], (PAIR_HID, C_PAIR), PAIR_HID ** -0.5, 0.375)
    w_bias = scatter_about(key_list[14], (C_PAIR, TOK_HEADS), 0.25, 1.5)
    w_back = scatter_about(key_list[15], (C_TOK, C_ATOM), C_TOK ** -0.5, 0.21875)
    return dict(atom_feat=atom_feat, atom_token=atom_token, atom_count=atom_count, window_start=window_start, w_atom_qkv=w_atom_qkv, w_atom_out=w_atom_out, w_atom_tok=w_atom_tok, single=single, tok_gain=tok_gain, w_tok=w_tok, w_tok_out=w_tok_out, pair=pair, w_pair_in=w_pair_in, w_pair_out=w_pair_out, w_bias=w_bias, w_back=w_back)


eps = 1e-05

def layer_norm(values):
    average = lax.optimization_barrier(jnp.mean(values, axis=-1, keepdims=True))
    centred = values - average
    spread = lax.optimization_barrier(jnp.mean(centred * centred, axis=-1, keepdims=True))
    return centred * lax.rsqrt(spread + eps)

def window_attention(queries, keys_values, present, starts):
    capacity, feat_width = queries.shape
    blocks = capacity // QUERY_BLOCK
    head_dim = feat_width // ATOM_HEADS

    def cut_window(offset):
        return (lax.dynamic_slice_in_dim(keys_values, offset, KEY_WINDOW, 0), lax.dynamic_slice_in_dim(present, offset, KEY_WINDOW, 0))
    windows, allowed = jax.vmap(cut_window)(starts)
    key_rows = windows[:, :, :feat_width].astype(jnp.float32).reshape(blocks, KEY_WINDOW, ATOM_HEADS, head_dim)
    value_rows = windows[:, :, feat_width:].astype(jnp.float32).reshape(blocks, KEY_WINDOW, ATOM_HEADS, head_dim)
    grouped = queries.astype(jnp.float32).reshape(blocks, QUERY_BLOCK, ATOM_HEADS, head_dim)
    scores = jnp.einsum('bqhd,bkhd->bhqk', grouped, key_rows) / math.sqrt(head_dim)
    scores = jnp.where(allowed[:, None, None, :], scores, -1e+30)
    row_max = lax.optimization_barrier(jnp.max(scores, axis=-1, keepdims=True))
    weights = jnp.exp(scores - row_max)
    weight_sum = lax.optimization_barrier(jnp.sum(weights, axis=-1))
    rounded = lax.optimization_barrier(weights.astype(jnp.bfloat16)).astype(jnp.float32)
    blended = jnp.einsum('bhqk,bkhd->bqhd', rounded, value_rows)
    blended = blended / jnp.transpose(weight_sum, (0, 2, 1))[:, :, :, None]
    return blended.reshape(capacity, feat_width).astype(jnp.bfloat16)

def one_block(features, prev_tail, next_head, live_count, starts, block_index, blocks_total, w_atom_qkv, w_atom_out):
    capacity, feat_width = features.shape
    halo_before = prev_tail.shape[0]
    halo_after = next_head.shape[0]
    ext_length = halo_before + capacity + halo_after
    extended = jnp.zeros((ext_length, feat_width), features.dtype)
    extended = lax.dynamic_update_slice_in_dim(extended, prev_tail, 0, 0)
    extended = lax.dynamic_update_slice_in_dim(extended, features, halo_before, 0)
    extended = lax.dynamic_update_slice_in_dim(extended, next_head, (halo_before + live_count).astype(jnp.int32), 0)
    positions = jnp.arange(ext_length, dtype=jnp.int32)
    present = ((positions >= halo_before) | (block_index > 0)) & ((positions < halo_before + live_count) | (positions < halo_before + live_count + halo_after) & (block_index < blocks_total - 1))
    queries = jnp.dot(features, w_atom_qkv[:, :feat_width], preferred_element_type=jnp.float32).astype(jnp.bfloat16)
    keys_values = jnp.dot(extended, w_atom_qkv[:, feat_width:], preferred_element_type=jnp.float32).astype(jnp.bfloat16)
    blended = window_attention(queries, keys_values, present, (starts + halo_before).astype(jnp.int32))
    return (features.astype(jnp.float32) + jnp.dot(blended, w_atom_out, preferred_element_type=jnp.float32)).astype(jnp.bfloat16)

def pair_piece(pair_tile, w_pair_in, w_pair_out, w_bias):
    tile_rows, tile_cols, channels = pair_tile.shape
    flat_tile = pair_tile.reshape(tile_rows * tile_cols, channels)
    normed = layer_norm(flat_tile.astype(jnp.float32)).astype(jnp.bfloat16)
    gate_up = jnp.dot(normed, w_pair_in, preferred_element_type=jnp.float32)
    hidden_width = w_pair_out.shape[0]
    hidden = (jax.nn.silu(gate_up[:, :hidden_width]) * gate_up[:, hidden_width:]).astype(jnp.bfloat16)
    updated = (flat_tile.astype(jnp.float32) + jnp.dot(hidden, w_pair_out, preferred_element_type=jnp.float32)).astype(jnp.bfloat16)
    renormed = layer_norm(updated.astype(jnp.float32)).astype(jnp.bfloat16)
    pair_bias = jnp.einsum('kh,pk->hp', w_bias.astype(jnp.float32), renormed.astype(jnp.float32)).astype(jnp.bfloat16)
    return (updated.reshape(tile_rows, tile_cols, channels), pair_bias.reshape(-1, tile_rows, tile_cols))

def attend(queries, keys_values, pair_bias):
    rows_here, feat_width = queries.shape
    head_dim = feat_width // TOK_HEADS
    query_rows = queries.astype(jnp.float32).reshape(rows_here, TOK_HEADS, head_dim)
    key_rows = keys_values[:, :feat_width].astype(jnp.float32).reshape(-1, TOK_HEADS, head_dim)
    value_rows = keys_values[:, feat_width:].astype(jnp.float32).reshape(-1, TOK_HEADS, head_dim)
    scores = jnp.einsum('ihd,jhd->hij', query_rows, key_rows) / math.sqrt(head_dim) + pair_bias.astype(jnp.float32)
    row_max = lax.optimization_barrier(jnp.max(scores, axis=-1, keepdims=True))
    weights = jnp.exp(scores - row_max)
    weight_sum = lax.optimization_barrier(jnp.sum(weights, axis=-1))
    rounded = lax.optimization_barrier(weights.astype(jnp.bfloat16)).astype(jnp.float32)
    blended = jnp.einsum('hij,jhd->ihd', rounded, value_rows)
    return (blended / jnp.transpose(weight_sum)[:, :, None]).reshape(rows_here, feat_width)

def reference(atom_feat, atom_token, atom_count, window_start, w_atom_qkv, w_atom_out, w_atom_tok, single, tok_gain, w_tok, w_tok_out, pair, w_pair_in, w_pair_out, w_bias, w_back):
    blocks_total = ATOMS // ATOM_CAP
    halo_before = KEY_WINDOW // 2
    halo_after = KEY_WINDOW - QUERY_BLOCK
    atom_blocks = atom_feat.reshape(blocks_total, ATOM_CAP, C_ATOM)
    counts = atom_count.astype(jnp.int32)

    def last_rows(features, live_count):
        return lax.dynamic_slice_in_dim(features, (live_count - halo_before).astype(jnp.int32), halo_before, 0)
    tail_rows = jax.vmap(last_rows)(atom_blocks, counts)
    head_rows = atom_blocks[:, :halo_after]
    prev_tail = jnp.concatenate([jnp.zeros((1, halo_before, C_ATOM), atom_feat.dtype), tail_rows[:-1]], axis=0)
    next_head = jnp.concatenate([head_rows[1:], jnp.zeros((1, halo_after, C_ATOM), atom_feat.dtype)], axis=0)
    block_ids = jnp.arange(blocks_total, dtype=jnp.int32)
    starts = window_start.astype(jnp.int32).reshape(blocks_total, ATOM_CAP // QUERY_BLOCK)
    per_block = partial(one_block, blocks_total=blocks_total, w_atom_qkv=w_atom_qkv, w_atom_out=w_atom_out)
    atom_mid = jax.vmap(per_block)(atom_blocks, prev_tail, next_head, counts, starts, block_ids).reshape(ATOMS, C_ATOM)
    live_slot = (jnp.arange(ATOM_CAP, dtype=jnp.int32)[None, :] < counts[:, None]).reshape(ATOMS)
    lifted = jax.nn.relu(jnp.dot(atom_mid, w_atom_tok, preferred_element_type=jnp.float32)).astype(jnp.bfloat16)
    pooled = jax.ops.segment_sum(jnp.where(live_slot[:, None], lifted.astype(jnp.float32), 0.0), atom_token, num_segments=TOKENS)
    members = jax.ops.segment_sum(live_slot.astype(jnp.float32), atom_token, num_segments=TOKENS)
    tok_state = single.astype(jnp.float32) + pooled / members[:, None]
    normed_tok = (layer_norm(tok_state) * tok_gain).astype(jnp.bfloat16)
    projected = jnp.dot(normed_tok, w_tok, preferred_element_type=jnp.float32).astype(jnp.bfloat16)
    queries = projected[:, :C_TOK]
    keys_values = projected[:, C_TOK:3 * C_TOK]
    gate_cols = projected[:, 3 * C_TOK:]

    def row_block(block_number):
        offset = (block_number * TOK_DEV).astype(jnp.int32)
        pair_tile = lax.dynamic_slice_in_dim(pair, offset, TOK_DEV, 0)
        updated, pair_bias = pair_piece(pair_tile, w_pair_in, w_pair_out, w_bias)
        blended = attend(lax.dynamic_slice_in_dim(queries, offset, TOK_DEV, 0), keys_values, pair_bias)
        return (updated, blended)
    updated, blended = lax.map(row_block, jnp.arange(TOKENS // TOK_DEV, dtype=jnp.int32))
    pair_out = updated.reshape(TOKENS, TOKENS, C_PAIR)
    token_mixed = blended.reshape(TOKENS, C_TOK)
    gated_mix = (token_mixed * jax.nn.sigmoid(gate_cols.astype(jnp.float32))).astype(jnp.bfloat16)
    token_out = (tok_state + jnp.dot(gated_mix, w_tok_out, preferred_element_type=jnp.float32)).astype(jnp.bfloat16)
    chosen = token_out[atom_token]
    atom_out = jnp.where(live_slot[:, None], atom_mid.astype(jnp.float32) + jnp.dot(chosen, w_back, preferred_element_type=jnp.float32), 0.0).astype(jnp.bfloat16)
    return (token_out, atom_out, pair_out)
```

```python
import functools
import math

import jax
import jax.numpy as jnp
from jax import lax
from jax.experimental import pallas as pl
from jax.experimental.pallas import tpu as pltpu
from jax.sharding import PartitionSpec as P

ATOM_HEADS = 4
TOK_HEADS = 16
QUERY_BLOCK = 32
KEY_WINDOW = 128
BEFORE = KEY_WINDOW // 2
AFTER = KEY_WINDOW - QUERY_BLOCK
CAP = 256
TOK_DEV = 16
C_ATOM = 128
C_TOK = 768
C_PAIR = 128
HID = 256
ROWS = 8
COLS = 16
TILE_I = 256
TILE_J = 128
MESSAGE = C_TOK + 128
EPS = 1e-05

f32 = jnp.float32
bf16 = jnp.bfloat16
MESH = pl.DeviceIdType.MESH
VMEM = pl.BlockSpec(memory_space=pltpu.VMEM)
SMEM = pl.BlockSpec(memory_space=pltpu.SMEM)
ANY = pl.BlockSpec(memory_space=pl.ANY)


def dot(a, b):
    return jnp.dot(a, b, preferred_element_type=f32)


def dot_nt(a, b):
    return lax.dot_general(a, b, (((1,), (1,)), ((), ())), preferred_element_type=f32)


def iota(shape, dim):
    return lax.broadcasted_iota(jnp.int32, shape, dim)


def shifted(block, axis, distance):
    devices = range(lax.axis_size(axis))
    route = [(i - distance, i) for i in devices if i - distance in devices]
    return lax.ppermute(block, axis, route)


def membership(token, live_count, block):
    shape = (TOK_DEV, CAP)
    local = token - block * TOK_DEV
    return ((iota(shape, 0) == local) & (iota(shape, 1) < live_count)).astype(f32)


def atom_kernel(
    count_ref, starts_ref, feat_ref, tail_ref, head_ref, token_ref, w_qkv_ref, w_out_ref, w_lift_ref,
    single_ref, gain_ref, w_tok_ref, mid_ref, state_ref, query_ref, kv_ref, gate_ref,
):
    block = lax.axis_index("row") * COLS + lax.axis_index("col")
    last = ROWS * COLS - 1
    count = count_ref[0]
    feat = feat_ref[...]
    rows = jnp.concatenate([tail_ref[...], feat, head_ref[...]], axis=0)
    length = rows.shape[0]
    queries = dot(feat, w_qkv_ref[:, :C_ATOM]).astype(bf16)
    keys_values = dot(rows, w_qkv_ref[:, C_ATOM:]).astype(bf16)
    keys, values = keys_values[:, :C_ATOM], keys_values[:, C_ATOM:]
    index = iota((1, length), 1)
    absent = -(1 << 20)
    shift_tail = jnp.where(block > 0, 0, absent)
    shift_head = jnp.where(block < last, count - CAP, absent)
    shift_own = jnp.where(index < BEFORE + count, 0, absent)
    position = index + jnp.where(
        index < BEFORE, shift_tail, jnp.where(index < BEFORE + CAP, shift_own, shift_head)
    )
    window = iota((CAP, 1), 0) // QUERY_BLOCK
    start = jnp.zeros((CAP, 1), jnp.int32)
    for b in range(CAP // QUERY_BLOCK):
        start = jnp.where(window == b, starts_ref[b] + BEFORE, start)
    allowed = (position >= start) & (position < start + KEY_WINDOW)
    width = C_ATOM // ATOM_HEADS
    lane = iota((CAP, C_ATOM), 1)
    mixed = jnp.zeros((CAP, C_ATOM), f32)
    for h in range(ATOM_HEADS):
        mine = (lane >= h * width) & (lane < (h + 1) * width)
        scores = dot_nt(jnp.where(mine, queries, jnp.zeros_like(queries)), keys)
        scores = jnp.where(allowed, scores * (1.0 / math.sqrt(width)), -1e30)
        weights = jnp.exp(scores - jnp.max(scores, axis=1, keepdims=True))
        total = jnp.sum(weights, axis=1, keepdims=True)
        mixed = jnp.where(mine, dot(weights.astype(bf16), values) / total, mixed)
    mid = (feat.astype(f32) + dot(mixed.astype(bf16), w_out_ref[...])).astype(bf16)
    mid_ref[...] = mid
    lifted = jnp.maximum(dot(mid, w_lift_ref[...]), 0.0).astype(bf16)
    member = membership(token_ref[...], count, block)
    members = jnp.sum(member, axis=1, keepdims=True)
    state = single_ref[...].astype(f32) + dot(member.astype(bf16), lifted) / members
    state_ref[...] = state
    centred = state - jnp.mean(state, axis=1, keepdims=True)
    spread = jnp.mean(centred * centred, axis=1, keepdims=True)
    normed = (centred * lax.rsqrt(spread + EPS) * gain_ref[...]).astype(bf16)
    query_ref[...] = dot(normed, w_tok_ref[:, :C_TOK]).astype(bf16)
    kv_ref[...] = dot(normed, w_tok_ref[:, C_TOK : 3 * C_TOK]).astype(bf16)
    gate_ref[...] = dot(normed, w_tok_ref[:, 3 * C_TOK :]).astype(bf16)


def atom_part(count, starts, feat, tail, head, token, w_qkv, w_out, w_lift, single, gain, w_tok):
    return pl.pallas_call(
        atom_kernel,
        out_shape=[
            jax.ShapeDtypeStruct((CAP, C_ATOM), bf16),
            jax.ShapeDtypeStruct((TOK_DEV, C_TOK), f32),
            jax.ShapeDtypeStruct((TOK_DEV, C_TOK), bf16),
            jax.ShapeDtypeStruct((TOK_DEV, 2 * C_TOK), bf16),
            jax.ShapeDtypeStruct((TOK_DEV, C_TOK), bf16),
        ],
        in_specs=[SMEM, SMEM] + [VMEM] * 10,
        out_specs=[VMEM] * 5,
        compiler_params=pltpu.CompilerParams(vmem_limit_bytes=32 << 20),
        name="atom_part",
    )(count, starts, feat, tail, head, token, w_qkv, w_out, w_lift, single, gain, w_tok)


def exchange_kernel(query_ref, kv_ref, queries_ref, kvs_ref, q_send, q_recv, kv_send, kv_recv):
    r, c = lax.axis_index("row"), lax.axis_index("col")
    self_kv = c == 2 * r + c // 8
    barrier = pltpu.get_barrier_semaphore()

    def source(k):
        return c // 2, lax.rem(c, 2) * 8 + k

    for k in range(1, COLS):
        pl.semaphore_signal(
            barrier, inc=1, device_id=(r, lax.rem(c + k, COLS)), device_id_type=MESH
        )
    for k in range(ROWS):
        sr, sc = source(k)

        @pl.when((sr != r) | (sc != c))
        def _():
            pl.semaphore_signal(barrier, inc=1, device_id=(sr, sc), device_id_type=MESH)

    pl.semaphore_wait(barrier, COLS - 1 + ROWS - self_kv.astype(jnp.int32))

    def q_copy(k):
        return pltpu.make_async_remote_copy(
            src_ref=query_ref,
            dst_ref=queries_ref.at[c],
            send_sem=q_send.at[k],
            recv_sem=q_recv.at[c],
            device_id=(r, lax.rem(c + k, COLS)),
            device_id_type=MESH,
        )

    def q_arrival(k):
        s = lax.rem(c + k, COLS)
        return pltpu.make_async_remote_copy(
            src_ref=query_ref,
            dst_ref=queries_ref.at[s],
            send_sem=q_send.at[k],
            recv_sem=q_recv.at[s],
            device_id=(r, s),
            device_id_type=MESH,
        )

    def kv_copy(k):
        slot = lax.rem(c, 8)
        return pltpu.make_async_remote_copy(
            src_ref=kv_ref,
            dst_ref=kvs_ref.at[slot],
            send_sem=kv_send.at[k],
            recv_sem=kv_recv.at[slot],
            device_id=(k, 2 * r + c // 8),
            device_id_type=MESH,
        )

    def kv_arrival(k):
        sr, sc = source(k)
        return pltpu.make_async_remote_copy(
            src_ref=kv_ref,
            dst_ref=kvs_ref.at[k],
            send_sem=kv_send.at[k],
            recv_sem=kv_recv.at[k],
            device_id=(sr, sc),
            device_id_type=MESH,
        )

    def elsewhere(k):
        return (k != r) | (2 * r + c // 8 != c)

    for k in range(ROWS):

        @pl.when(elsewhere(k))
        def _():
            kv_copy(k).start()

    for k in range(1, COLS):
        q_copy(k).start()
    queries_ref[c] = query_ref[...]

    @pl.when(self_kv)
    def _():
        kvs_ref[lax.rem(c, 8)] = kv_ref[...]

    for k in range(ROWS):
        sr, sc = source(k)

        @pl.when((sr != r) | (sc != c))
        def _():
            kv_arrival(k).wait_recv()

        @pl.when(elsewhere(k))
        def _():
            kv_copy(k).wait_send()

    for k in range(1, COLS):
        q_arrival(k).wait_recv()
        q_copy(k).wait_send()


def exchange(query, kv):
    return pl.pallas_call(
        exchange_kernel,
        out_shape=[
            jax.ShapeDtypeStruct((COLS, TOK_DEV, C_TOK), bf16),
            jax.ShapeDtypeStruct((ROWS, TOK_DEV, 2 * C_TOK), bf16),
        ],
        in_specs=[VMEM] * 2,
        out_specs=[VMEM] * 2,
        scratch_shapes=[
            pltpu.SemaphoreType.DMA((COLS,)),
            pltpu.SemaphoreType.DMA((COLS,)),
            pltpu.SemaphoreType.DMA((ROWS,)),
            pltpu.SemaphoreType.DMA((ROWS,)),
        ],
        compiler_params=pltpu.CompilerParams(
            collective_id=0, has_side_effects=True, vmem_limit_bytes=16 << 20
        ),
        name="exchange",
    )(query, kv)


PAIR_ROWS = 32


def pair_kernel(
    pair_ref, w_in_ref, w_out_ref, w_bias_ref, out_ref, bias_ref, held, done, in_sem, out_sem, w_up, w_down
):
    pieces = TILE_I // PAIR_ROWS
    positions = PAIR_ROWS * TILE_J

    def rows(k):
        return pl.ds(k * PAIR_ROWS, PAIR_ROWS)

    def load(k):
        return pltpu.make_async_copy(pair_ref.at[rows(k)], held.at[rows(k)], in_sem.at[k])

    def store(k):
        return pltpu.make_async_copy(done.at[rows(k)], out_ref.at[rows(k)], out_sem.at[k])

    for k in range(pieces):
        load(k).start()
    w_in = w_in_ref[...].astype(f32)
    w_up[:HID] = (w_in[:, :HID].T * 0.5).astype(bf16)
    w_up[HID : 2 * HID] = w_in[:, HID:].T.astype(bf16)
    w_bias = w_bias_ref[...].astype(f32).T
    w_up[2 * HID :] = w_bias.astype(bf16)
    w_down[:C_PAIR] = w_out_ref[...].astype(f32).T.astype(bf16)
    w_down[C_PAIR:] = lax.dot_general(
        w_bias_ref[...], w_out_ref[...], (((0,), (1,)), ((), ())), preferred_element_type=f32
    ).astype(bf16)
    bias_sum = jnp.sum(w_bias, axis=1, keepdims=True)
    share = 1.0 / C_PAIR

    def step(k, carry):
        load(k).wait()
        tile = held[rows(k)].reshape(positions, C_PAIR).T
        wide = tile.astype(f32)
        mean = jnp.sum(wide, axis=0, keepdims=True) * share
        centred = wide - mean
        spread = jnp.sum(centred * centred, axis=0, keepdims=True) * share + EPS
        scale = lax.rsqrt(spread)
        up = dot(w_up[...], (centred * scale).astype(bf16))
        gate, value = up[:HID].astype(bf16), up[HID : 2 * HID].astype(bf16)
        hidden = (gate + gate * jnp.tanh(gate)) * value
        down = dot(w_down[...], hidden)
        updated = (wide + down[:C_PAIR]).astype(bf16)
        done[rows(k)] = updated.T.reshape(PAIR_ROWS, TILE_J, C_PAIR)
        store(k).start()
        again = updated.astype(f32)
        mean_again = jnp.sum(again, axis=0, keepdims=True) * share
        centred = again - mean_again
        spread_again = jnp.sum(centred * centred, axis=0, keepdims=True) * share + EPS
        bias = up[2 * HID :] * (spread * scale) + down[C_PAIR:] + bias_sum * (mean - mean_again)
        bias = (bias * lax.rsqrt(spread_again)).astype(bf16)
        for i in range(PAIR_ROWS):
            bias_ref[k * PAIR_ROWS + i] = bias[:, i * TILE_J : (i + 1) * TILE_J]
        return carry

    lax.fori_loop(0, pieces, step, 0)
    for k in range(pieces):
        store(k).wait()


def pair_part(pair, w_in, w_out, w_bias):
    pieces = TILE_I // PAIR_ROWS
    return pl.pallas_call(
        pair_kernel,
        out_shape=[
            jax.ShapeDtypeStruct(pair.shape, bf16),
            jax.ShapeDtypeStruct((TILE_I, TOK_HEADS, TILE_J), bf16),
        ],
        in_specs=[ANY, VMEM, VMEM, VMEM],
        out_specs=[ANY, VMEM],
        scratch_shapes=[
            pltpu.VMEM((TILE_I, TILE_J, C_PAIR), bf16),
            pltpu.VMEM((TILE_I, TILE_J, C_PAIR), bf16),
            pltpu.SemaphoreType.DMA((pieces,)),
            pltpu.SemaphoreType.DMA((pieces,)),
            pltpu.VMEM((2 * HID + TOK_HEADS, C_PAIR), bf16),
            pltpu.VMEM((C_PAIR + TOK_HEADS, HID), bf16),
        ],
        compiler_params=pltpu.CompilerParams(vmem_limit_bytes=48 << 20),
        name="pair_part",
    )(pair, w_in, w_out, w_bias)


def attend_kernel(
    count_ref, queries_ref, kvs_ref, bias_ref, gate_ref, state_ref, mid_ref, token_ref, w_tok_out_ref, w_back_ref,
    token_out_ref, atom_out_ref, outbox, inbox, send_sem, recv_sem,
):
    r, c = lax.axis_index("row"), lax.axis_index("col")
    block = r * COLS + c
    width = C_TOK // TOK_HEADS
    barrier = pltpu.get_barrier_semaphore()
    for k in range(1, COLS):
        pl.semaphore_signal(
            barrier, inc=1, device_id=(r, lax.rem(c + k, COLS)), device_id_type=MESH
        )
    pl.semaphore_wait(barrier, COLS - 1)

    def copy(k):
        to = lax.rem(c + k, COLS)
        return pltpu.make_async_remote_copy(
            src_ref=outbox.at[to],
            dst_ref=inbox.at[c],
            send_sem=send_sem.at[to],
            recv_sem=recv_sem.at[c],
            device_id=(r, to),
            device_id_type=MESH,
        )

    def arrival(k):
        s = lax.rem(c + k, COLS)
        return pltpu.make_async_remote_copy(
            src_ref=outbox.at[s],
            dst_ref=inbox.at[s],
            send_sem=send_sem.at[s],
            recv_sem=recv_sem.at[s],
            device_id=(r, s),
            device_id_type=MESH,
        )

    head = iota((TOK_HEADS, C_TOK), 0) * width
    column = iota((TOK_HEADS, C_TOK), 1)
    in_head = (column >= head) & (column < head + width)
    head_one = in_head.astype(bf16)
    head_one_wide = in_head.astype(f32)
    lane_pick = (iota((TOK_HEADS, 128), 0) == iota((TOK_HEADS, 128), 1)).astype(f32)
    kvs = kvs_ref[...].reshape(TILE_J, 2 * C_TOK)
    keys, values = kvs[:, :C_TOK], kvs[:, C_TOK:]

    def partial(to):
        spread = queries_ref[to][:, None, :] * head_one[None]
        scores = dot_nt(spread.reshape(TOK_DEV * TOK_HEADS, C_TOK), keys)
        bias = bias_ref[pl.ds(to * TOK_DEV, TOK_DEV)].reshape(TOK_DEV * TOK_HEADS, TILE_J)
        scores = scores * (1.0 / math.sqrt(width)) + bias.astype(f32)
        top = jnp.max(scores, axis=1, keepdims=True).astype(bf16).astype(f32)
        weights = jnp.exp(scores - top)
        total = jnp.sum(weights, axis=1, keepdims=True)
        mixed = dot(weights.astype(bf16), values).reshape(TOK_DEV, TOK_HEADS, C_TOK)
        mixed = jnp.sum(mixed * head_one_wide[None], axis=1)

        def to_lanes(column_values):
            wide = jnp.broadcast_to(column_values, (TOK_DEV * TOK_HEADS, 128))
            return jnp.sum(wide.reshape(TOK_DEV, TOK_HEADS, 128) * lane_pick[None], axis=1)

        tops = to_lanes(top)[:, :TOK_HEADS]
        totals = to_lanes(total)[:, :TOK_HEADS]
        high = totals.astype(bf16)
        low = (totals - high.astype(f32)).astype(bf16)
        return mixed.astype(bf16), tops.astype(bf16), high, low

    def put(box, at, parts):
        mixed, tops, high, low = parts
        rest = jnp.zeros((TOK_DEV, 128 - 3 * TOK_HEADS), bf16)
        box[at, :, :C_TOK] = mixed
        box[at, :, C_TOK:] = jnp.concatenate([tops, high, low, rest], axis=1)

    def one(k, carry):
        to = lax.rem(c + k, COLS)
        put(outbox, to, partial(to))
        copy(k).start()
        return carry

    lax.fori_loop(1, COLS, one, 0)
    put(inbox, c, partial(c))

    def arrived(k, carry):
        arrival(k).wait_recv()
        copy(k).wait_send()
        return carry

    lax.fori_loop(1, COLS, arrived, 0)
    n = TOK_HEADS
    tails = [inbox[s, :, C_TOK:].astype(f32) for s in range(COLS)]
    tops = [t[:, :n] for t in tails]
    totals = [t[:, n : 2 * n] + t[:, 2 * n : 3 * n] for t in tails]
    top = functools.reduce(jnp.maximum, tops)
    factors = [jnp.exp(t - top) for t in tops]
    total = sum(f * t for f, t in zip(factors, totals))
    factors = jnp.concatenate([f / total for f in factors], axis=0)
    high = factors.astype(bf16)
    low = (factors - high.astype(f32)).astype(bf16)
    factors = dot(high, head_one) + dot(low, head_one)
    mixed = sum(
        factors[s * TOK_DEV : (s + 1) * TOK_DEV] * inbox[s, :, :C_TOK].astype(f32)
        for s in range(COLS)
    )
    gated = (mixed * jax.nn.sigmoid(gate_ref[...].astype(f32))).astype(bf16)
    token_out = (state_ref[...] + dot(gated, w_tok_out_ref[...])).astype(bf16)
    token_out_ref[...] = token_out
    count = count_ref[0]
    member = membership(token_ref[...], count, block).astype(bf16)
    same = (iota((CAP, CAP), 0) == iota((CAP, CAP), 1)).astype(bf16)
    chosen = dot(dot_nt(same, member).astype(bf16), token_out).astype(bf16)
    back = mid_ref[...].astype(f32) + dot(chosen, w_back_ref[...])
    atom_out_ref[...] = jnp.where(iota((CAP, 1), 0) < count, back, 0.0).astype(bf16)


def attend_part(count, queries, kvs, bias, gate, state, mid, token, w_tok_out, w_back):
    return pl.pallas_call(
        attend_kernel,
        out_shape=[
            jax.ShapeDtypeStruct((TOK_DEV, C_TOK), bf16),
            jax.ShapeDtypeStruct((CAP, C_ATOM), bf16),
        ],
        in_specs=[SMEM] + [VMEM] * 9,
        out_specs=[VMEM] * 2,
        scratch_shapes=[
            pltpu.VMEM((COLS, TOK_DEV, MESSAGE), bf16),
            pltpu.VMEM((COLS, TOK_DEV, MESSAGE), bf16),
            pltpu.SemaphoreType.DMA((COLS,)),
            pltpu.SemaphoreType.DMA((COLS,)),
        ],
        compiler_params=pltpu.CompilerParams(
            collective_id=1, has_side_effects=True, vmem_limit_bytes=32 << 20
        ),
        name="attend_part",
    )(count, queries, kvs, bias, gate, state, mid, token, w_tok_out, w_back)


def local(
    atom_feat,
    atom_token,
    atom_count,
    window_start,
    w_atom_qkv,
    w_atom_out,
    w_atom_tok,
    single,
    tok_gain,
    w_tok,
    w_tok_out,
    pair,
    w_pair_in,
    w_pair_out,
    w_bias,
    w_back,
):
    tail = lax.dynamic_slice_in_dim(atom_feat, atom_count[0] - BEFORE, BEFORE, 0)
    prev_tail = shifted(tail, ("row", "col"), 1)
    next_head = shifted(atom_feat[:AFTER], ("row", "col"), -1)
    token = atom_token.reshape(1, CAP)
    mid, state, query, kv, gate = atom_part(
        atom_count, window_start, atom_feat, prev_tail, next_head, token, w_atom_qkv, w_atom_out,
        w_atom_tok, single, tok_gain.reshape(1, C_TOK), w_tok,
    )
    queries, kvs = exchange(query, kv)
    pair_out, bias = pair_part(pair, w_pair_in, w_pair_out, w_bias)
    token_out, atom_out = attend_part(
        atom_count, queries, kvs, bias, gate, state, mid, token, w_tok_out, w_back
    )
    return (token_out, atom_out, pair_out)


def solution(mesh):
    tokens = P(("row", "col"), None)
    flat = P(("row", "col"))
    return jax.shard_map(
        local,
        mesh=mesh,
        in_specs=(
            tokens, flat, flat, flat, P(), P(), P(), tokens, P(), P(), P(), P("row", "col", None),
            P(), P(), P(), P(),
        ),
        out_specs=(tokens, tokens, P("row", "col", None)),
        check_vma=False,
    )
```

```python
import functools
import math

import jax
import jax.numpy as jnp
from jax import lax
from jax.experimental import pallas as pl
from jax.experimental.pallas import tpu as pltpu
from jax.sharding import PartitionSpec as P

ATOM_HEADS = 4
TOK_HEADS = 16
QUERY_BLOCK = 32
KEY_WINDOW = 128
BEFORE = KEY_WINDOW // 2
AFTER = KEY_WINDOW - QUERY_BLOCK
CAP = 256
TOK_DEV = 16
C_ATOM = 128
C_TOK = 768
C_PAIR = 128
HID = 256
ROWS = 8
COLS = 16
TILE_I = 256
TILE_J = 128
MESSAGE = C_TOK + 128
EPS = 1e-05

f32 = jnp.float32
bf16 = jnp.bfloat16
MESH = pl.DeviceIdType.MESH
VMEM = pl.BlockSpec(memory_space=pltpu.VMEM)
SMEM = pl.BlockSpec(memory_space=pltpu.SMEM)
ANY = pl.BlockSpec(memory_space=pl.ANY)
HBM = pl.BlockSpec(memory_space=pltpu.HBM)


def dot(a, b):
    return jnp.dot(a, b, preferred_element_type=f32)


def dot_nt(a, b):
    return lax.dot_general(a, b, (((1,), (1,)), ((), ())), preferred_element_type=f32)


def iota(shape, dim):
    return lax.broadcasted_iota(jnp.int32, shape, dim)


def membership(token, live_count, block):
    shape = (TOK_DEV, CAP)
    local = token - block * TOK_DEV
    return ((iota(shape, 0) == local) & (iota(shape, 1) < live_count)).astype(f32)


CHUNK = 32
CHUNKS = TILE_I // CHUNK
EARLY = 1
BEFORE_ATTEND = 5
WINDOWS = (0, 128, 384, 512)
WIDE = 256
GROUP = 4


def atom_attention(block, count, starts_ref, feat, tail, head, w_qkv_ref, w_out_ref):
    last = ROWS * COLS - 1
    rows = jnp.concatenate([tail, feat, head], axis=0)
    length = rows.shape[0]
    queries = dot(feat, w_qkv_ref[:, :C_ATOM]).astype(bf16)
    keys_values = dot(rows, w_qkv_ref[:, C_ATOM:]).astype(bf16)
    keys, values = keys_values[:, :C_ATOM], keys_values[:, C_ATOM:]
    index = iota((1, length), 1)
    absent = -(1 << 20)
    shift_tail = jnp.where(block > 0, 0, absent)
    shift_head = jnp.where(block < last, count - CAP, absent)
    shift_own = jnp.where(index < BEFORE + count, 0, absent)
    position = index + jnp.where(
        index < BEFORE, shift_tail, jnp.where(index < BEFORE + CAP, shift_own, shift_head)
    )
    window = iota((CAP, 1), 0) // QUERY_BLOCK
    start = jnp.zeros((CAP, 1), jnp.int32)
    for b in range(CAP // QUERY_BLOCK):
        start = jnp.where(window == b, starts_ref[b] + BEFORE, start)
    allowed = (position >= start) & (position < start + KEY_WINDOW)
    width = C_ATOM // ATOM_HEADS
    lane = iota((CAP, C_ATOM), 1)
    mixed = jnp.zeros((CAP, C_ATOM), f32)
    for h in range(ATOM_HEADS):
        mine = (lane >= h * width) & (lane < (h + 1) * width)
        scores = dot_nt(jnp.where(mine, queries, jnp.zeros_like(queries)), keys)
        scores = jnp.where(allowed, scores * (1.0 / math.sqrt(width)), -1e30)
        weights = jnp.exp(scores - jnp.max(scores, axis=1, keepdims=True))
        total = jnp.sum(weights, axis=1, keepdims=True)
        mixed = jnp.where(mine, dot(weights.astype(bf16), values) / total, mixed)
    return (feat.astype(f32) + dot(mixed.astype(bf16), w_out_ref[...])).astype(bf16)


def main_kernel(
    count_ref, starts_hbm, feat_hbm, token_hbm, w_qkv_hbm, w_out_hbm, w_lift_hbm, single_hbm, gain_hbm, w_tok_hbm,
    pair_hbm, w_in_hbm, w_pair_out_hbm, w_bias_hbm,
    done, inbox, mid_ref, state_ref, gate_ref,
    starts_ref, feat_ref, token_ref, w_qkv_ref, w_out_ref, w_lift_ref, single_ref, gain_ref, w_tok_ref, w_in_ref, w_pair_out_ref,
    w_bias_ref, load_sem, held, pair_sem, w_up, w_down, bias_ref, tail_out, tail_ref, head_ref, halo_send, halo_recv,
    query_ref, kv_ref, queries_ref, kvs_ref, q_send, q_recv, kv_send, kv_recv, outbox, out_send, out_recv,
):
    r, c = lax.axis_index("row"), lax.axis_index("col")
    block = r * COLS + c
    last = ROWS * COLS - 1
    count = count_ref[0]
    sides = [
        (feat_hbm, feat_ref), (w_in_hbm, w_in_ref), (w_pair_out_hbm, w_pair_out_ref), (w_bias_hbm, w_bias_ref),
        (w_qkv_hbm, w_qkv_ref), (w_out_hbm, w_out_ref), (w_lift_hbm, w_lift_ref), (token_hbm, token_ref),
        (single_hbm, single_ref), (starts_hbm, starts_ref), (gain_hbm, gain_ref), (w_tok_hbm, w_tok_ref),
    ]
    loads = [
        pltpu.make_async_copy(src, dst, load_sem.at[n]) for n, (src, dst) in enumerate(sides)
    ]

    def chunk_at(t):
        return lax.rem(c // 2 + 1 + t, CHUNKS)

    def pair_load(t):
        k = chunk_at(t)
        rows = pl.ds(k * CHUNK, CHUNK)
        return pltpu.make_async_copy(pair_hbm.at[rows], held.at[rows], pair_sem.at[k])

    for load in loads[:4]:
        load.start()
    pair_load(0).start()
    for load in loads[4:]:
        load.start()
    for t in range(1, CHUNKS):
        pair_load(t).start()

    barrier = pltpu.get_barrier_semaphore()

    def greet(row, col):
        pl.semaphore_signal(barrier, inc=1, device_id=(row, col), device_id_type=MESH)

    def beside(distance):
        other = block + distance
        return other // COLS, lax.rem(other, COLS)

    def kv_source(k):
        return c // 2, lax.rem(c, 2) * ROWS + k

    def kv_target(k):
        return k, 2 * r + c // ROWS

    kv_here = c == 2 * r + c // ROWS

    def elsewhere(device):
        return (device[0] != r) | (device[1] != c)

    @pl.when(block > 0)
    def _():
        greet(*beside(-1))

    @pl.when(block < last)
    def _():
        greet(*beside(1))

    for k in range(1, COLS):
        greet(r, lax.rem(c + k, COLS))
    for k in range(ROWS):

        @pl.when(elsewhere(kv_source(k)))
        def _():
            greet(*kv_source(k))

    heard = (block > 0).astype(jnp.int32) + (block < last).astype(jnp.int32)
    pl.semaphore_wait(barrier, COLS - 1 + ROWS - kv_here.astype(jnp.int32) + heard)

    loads[0].wait()
    pick = iota((BEFORE, CAP), 1) == iota((BEFORE, CAP), 0) + (count - BEFORE)
    tail_out[...] = dot(pick.astype(bf16), feat_ref[...]).astype(bf16)

    def halo_copy(n, src, dst, distance):
        return pltpu.make_async_remote_copy(
            src_ref=src,
            dst_ref=dst,
            send_sem=halo_send.at[n],
            recv_sem=halo_recv.at[n],
            device_id=beside(distance),
            device_id_type=MESH,
        )

    def tail_copy():
        return halo_copy(0, tail_out, tail_ref, 1)

    def head_copy():
        return halo_copy(1, feat_ref.at[pl.ds(0, AFTER)], head_ref, -1)

    @pl.when(block < last)
    def _():
        tail_copy().start()

    @pl.when(block > 0)
    def _():
        head_copy().start()

    @pl.when(block == 0)
    def _():
        tail_ref[...] = jnp.zeros_like(tail_ref)

    @pl.when(block == last)
    def _():
        head_ref[...] = jnp.zeros_like(head_ref)

    for load in loads[1:4]:
        load.wait()
    w_in = w_in_ref[...].astype(f32)
    w_up[:HID] = (w_in[:, :HID].T * 0.5).astype(bf16)
    w_up[HID : 2 * HID] = w_in[:, HID:].T.astype(bf16)
    w_up[2 * HID :] = w_bias_ref[...]
    w_down[:C_PAIR] = w_pair_out_ref[...].astype(f32).T.astype(bf16)
    w_down[C_PAIR:] = dot_nt(w_bias_ref[...], w_pair_out_ref[...]).astype(bf16)
    bias_sum = jnp.sum(w_bias_ref[...].astype(f32), axis=1, keepdims=True)
    share = 1.0 / C_PAIR

    def pair_step(t):
        pair_load(t).wait()
        k = chunk_at(t)
        rows = pl.ds(k * CHUNK, CHUNK)
        tile = held[rows].reshape(CHUNK * TILE_J, C_PAIR).T
        wide = tile.astype(f32)
        mean = jnp.sum(wide, axis=0, keepdims=True) * share
        centred = wide - mean
        spread = jnp.sum(centred * centred, axis=0, keepdims=True) * share + EPS
        scale = lax.rsqrt(spread)
        up = dot(w_up[...], (centred * scale).astype(bf16))
        gate, value = up[:HID].astype(bf16), up[HID : 2 * HID].astype(bf16)
        hidden = (gate + gate * jnp.tanh(gate)) * value
        down = dot(w_down[...], hidden)
        updated = (wide + down[:C_PAIR]).astype(bf16)
        done[rows] = updated.T.reshape(CHUNK, TILE_J, C_PAIR)
        again = updated.astype(f32)
        mean_again = jnp.sum(again, axis=0, keepdims=True) * share
        centred = again - mean_again
        spread_again = jnp.sum(centred * centred, axis=0, keepdims=True) * share + EPS
        bias = up[2 * HID :] * (spread * scale) + down[C_PAIR:] + bias_sum * (mean - mean_again)
        bias = bias * lax.rsqrt(spread_again)
        for i in range(CHUNK):
            bias_ref[k, pl.ds(i, TOK_HEADS, stride=CHUNK), :] = bias[:, i * TILE_J : (i + 1) * TILE_J]

    def loop(first, stop, step):
        def body(t, carry):
            step(t)
            return carry

        lax.fori_loop(first, stop, body, 0)

    loop(0, EARLY, pair_step)

    @pl.when(block > 0)
    def _():
        halo_copy(0, tail_out, tail_ref, -1).wait_recv()
        head_copy().wait_send()

    @pl.when(block < last)
    def _():
        halo_copy(1, feat_ref.at[pl.ds(0, AFTER)], head_ref, 1).wait_recv()
        tail_copy().wait_send()

    for load in loads[4:]:
        load.wait()
    mid = atom_attention(
        block, count, starts_ref, feat_ref[...], tail_ref[...], head_ref[...], w_qkv_ref, w_out_ref
    )
    mid_ref[...] = mid
    lifted = jnp.maximum(dot(mid, w_lift_ref[...]), 0.0).astype(bf16)
    member = membership(token_ref[...], count, block)
    members = jnp.sum(member, axis=1, keepdims=True)
    state = single_ref[...].astype(f32) + dot(member.astype(bf16), lifted) / members
    state_ref[...] = state
    centred = state - jnp.mean(state, axis=1, keepdims=True)
    spread = jnp.mean(centred * centred, axis=1, keepdims=True)
    normed = (centred * lax.rsqrt(spread + EPS) * gain_ref[...].reshape(1, C_TOK)).astype(bf16)
    kv_ref[...] = dot(normed, w_tok_ref[:, C_TOK : 3 * C_TOK]).astype(bf16)

    def kv_copy(k):
        slot = lax.rem(c, ROWS)
        return pltpu.make_async_remote_copy(
            src_ref=kv_ref,
            dst_ref=kvs_ref.at[slot],
            send_sem=kv_send.at[k],
            recv_sem=kv_recv.at[slot],
            device_id=kv_target(k),
            device_id_type=MESH,
        )

    def kv_arrival(k):
        return pltpu.make_async_remote_copy(
            src_ref=kv_ref,
            dst_ref=kvs_ref.at[k],
            send_sem=kv_send.at[k],
            recv_sem=kv_recv.at[k],
            device_id=kv_source(k),
            device_id_type=MESH,
        )

    def q_copy(k):
        return pltpu.make_async_remote_copy(
            src_ref=query_ref,
            dst_ref=queries_ref.at[c],
            send_sem=q_send.at[k],
            recv_sem=q_recv.at[c],
            device_id=(r, lax.rem(c + k, COLS)),
            device_id_type=MESH,
        )

    def q_arrival(k):
        s = lax.rem(c + k, COLS)
        return pltpu.make_async_remote_copy(
            src_ref=query_ref,
            dst_ref=queries_ref.at[s],
            send_sem=q_send.at[k],
            recv_sem=q_recv.at[s],
            device_id=(r, s),
            device_id_type=MESH,
        )

    for k in range(ROWS):

        @pl.when(elsewhere(kv_target(k)))
        def _():
            kv_copy(k).start()

    query_ref[...] = dot(normed, w_tok_ref[:, :C_TOK]).astype(bf16)
    for k in range(1, COLS):
        q_copy(k).start()
    gate_ref[...] = dot(normed, w_tok_ref[:, 3 * C_TOK :]).astype(bf16)
    queries_ref[c] = query_ref[...]

    @pl.when(kv_here)
    def _():
        kvs_ref[lax.rem(c, ROWS)] = kv_ref[...]

    loop(EARLY, BEFORE_ATTEND, pair_step)

    for k in range(ROWS):

        @pl.when(elsewhere(kv_source(k)))
        def _():
            kv_arrival(k).wait_recv()

        @pl.when(elsewhere(kv_target(k)))
        def _():
            kv_copy(k).wait_send()

    for k in range(1, COLS):
        q_arrival(k).wait_recv()
        q_copy(k).wait_send()

    width = C_TOK // TOK_HEADS
    kvs = kvs_ref[...].reshape(TILE_J, 2 * C_TOK)
    column = iota((CHUNK, WIDE), 1)
    lane = iota((CHUNK, 128), 1)

    def out_copy(to):
        return pltpu.make_async_remote_copy(
            src_ref=outbox.at[to],
            dst_ref=inbox.at[c],
            send_sem=out_send.at[to],
            recv_sem=out_recv.at[c],
            device_id=(r, to),
            device_id_type=MESH,
        )

    def out_arrival(s):
        return pltpu.make_async_remote_copy(
            src_ref=outbox.at[s],
            dst_ref=inbox.at[s],
            send_sem=out_send.at[s],
            recv_sem=out_recv.at[s],
            device_id=(r, s),
            device_id_type=MESH,
        )

    def attend_step(t):
        k = chunk_at(t)
        pair_of = pl.ds(2 * k, 2)
        queries = queries_ref[pair_of].reshape(CHUNK, C_TOK)
        parts = []
        notes = jnp.zeros((CHUNK, 128), f32)
        for g, at in enumerate(WINDOWS):
            mine = [
                (column >= h * width - at) & (column < (h + 1) * width - at)
                for h in range(GROUP * g, GROUP * (g + 1))
            ]
            seen = queries[:, at : at + WIDE]
            stack = jnp.concatenate(
                [jnp.where(m, seen, jnp.zeros_like(seen)) for m in mine], axis=0
            )
            scores = dot_nt(stack, kvs[:, at : at + WIDE]) * (1.0 / math.sqrt(width))
            scores = scores + bias_ref[k, pl.ds(g * GROUP * CHUNK, GROUP * CHUNK), :]
            top = jnp.max(scores, axis=1, keepdims=True).astype(bf16).astype(f32)
            weights = jnp.exp(scores - top)
            total = jnp.sum(weights, axis=1, keepdims=True)
            mixed = dot(weights.astype(bf16), kvs[:, C_TOK + at : C_TOK + at + WIDE])
            part = jnp.zeros((CHUNK, WIDE), f32)
            for n, m in enumerate(mine):
                rows = slice(n * CHUNK, (n + 1) * CHUNK)
                part = jnp.where(m, mixed[rows], part)
                h = GROUP * g + n
                high = total[rows].astype(bf16).astype(f32)
                notes = jnp.where(lane == h, top[rows], notes)
                notes = jnp.where(lane == TOK_HEADS + h, high, notes)
                notes = jnp.where(lane == 2 * TOK_HEADS + h, total[rows] - high, notes)
            parts.append(part)
        half = WIDE // 2
        message = jnp.concatenate(
            [
                parts[0][:, :half], parts[0][:, half:] + parts[1][:, :half], parts[1][:, half:],
                parts[2][:, :half], parts[2][:, half:] + parts[3][:, :half], parts[3][:, half:], notes,
            ],
            axis=1,
        )
        outbox[pair_of] = message.astype(bf16).reshape(2, TOK_DEV, MESSAGE)
        for n in range(2):

            @pl.when(2 * k + n != c)
            def _():
                out_copy(2 * k + n).start()

    loop(0, BEFORE_ATTEND, attend_step)

    def both(t):
        pair_step(t)
        attend_step(t)

    loop(BEFORE_ATTEND, CHUNKS, both)
    inbox[c] = outbox[c]

    def arrived(k):
        s = lax.rem(c + k, COLS)
        out_arrival(s).wait_recv()
        out_copy(s).wait_send()

    loop(1, COLS, arrived)


def main_part(count, starts, feat, token, w_qkv, w_out, w_lift, single, gain, w_tok, pair, w_in, w_pair_out, w_bias):
    def vmem(*shape):
        return pltpu.VMEM(shape, bf16)

    def dma(n):
        return pltpu.SemaphoreType.DMA((n,))

    return pl.pallas_call(
        main_kernel,
        out_shape=[
            jax.ShapeDtypeStruct((TILE_I, TILE_J, C_PAIR), bf16),
            jax.ShapeDtypeStruct((COLS, TOK_DEV, MESSAGE), bf16),
            jax.ShapeDtypeStruct((CAP, C_ATOM), bf16),
            jax.ShapeDtypeStruct((TOK_DEV, C_TOK), f32),
            jax.ShapeDtypeStruct((TOK_DEV, C_TOK), bf16),
        ],
        in_specs=[SMEM] + [HBM] * 13,
        out_specs=[VMEM] * 5,
        scratch_shapes=[
            pltpu.SMEM((CAP // QUERY_BLOCK,), jnp.int32), vmem(CAP, C_ATOM), pltpu.VMEM((1, CAP), jnp.int32),
            vmem(C_ATOM, 3 * C_ATOM), vmem(C_ATOM, C_ATOM), vmem(C_ATOM, C_TOK), vmem(TOK_DEV, C_TOK),
            pltpu.VMEM((C_TOK,), f32), vmem(C_TOK, 4 * C_TOK), vmem(C_PAIR, 2 * HID), vmem(HID, C_PAIR),
            vmem(TOK_HEADS, C_PAIR), dma(12),
            vmem(TILE_I, TILE_J, C_PAIR), dma(CHUNKS),
            vmem(2 * HID + TOK_HEADS, C_PAIR), vmem(C_PAIR + TOK_HEADS, HID),
            pltpu.VMEM((CHUNKS, TOK_HEADS * CHUNK, TILE_J), f32),
            vmem(BEFORE, C_ATOM), vmem(BEFORE, C_ATOM), vmem(AFTER, C_ATOM), dma(2), dma(2),
            vmem(TOK_DEV, C_TOK), vmem(TOK_DEV, 2 * C_TOK),
            vmem(COLS, TOK_DEV, C_TOK), vmem(ROWS, TOK_DEV, 2 * C_TOK),
            dma(COLS), dma(COLS), dma(ROWS), dma(ROWS),
            vmem(COLS, TOK_DEV, MESSAGE), dma(COLS), dma(COLS),
        ],
        compiler_params=pltpu.CompilerParams(
            collective_id=0, has_side_effects=True, vmem_limit_bytes=36 << 20
        ),
        name="main_part",
    )(count, starts, feat, token, w_qkv, w_out, w_lift, single, gain, w_tok, pair, w_in, w_pair_out, w_bias)


def finish_kernel(
    count_ref, pair_ref, inbox, gate_ref, state_ref, mid_ref, token_ref, w_tok_out_ref, w_back_ref,
    token_out_ref, atom_out_ref, pair_out_ref, sem,
):
    write = pltpu.make_async_copy(pair_ref, pair_out_ref, sem)
    write.start()
    block = lax.axis_index("row") * COLS + lax.axis_index("col")
    width = C_TOK // TOK_HEADS
    head = iota((TOK_HEADS, C_TOK), 0) * width
    column = iota((TOK_HEADS, C_TOK), 1)
    head_one = ((column >= head) & (column < head + width)).astype(bf16)
    n = TOK_HEADS
    tails = [inbox[s, :, C_TOK:].astype(f32) for s in range(COLS)]
    tops = [t[:, :n] for t in tails]
    totals = [t[:, n : 2 * n] + t[:, 2 * n : 3 * n] for t in tails]
    top = functools.reduce(jnp.maximum, tops)
    factors = [jnp.exp(t - top) for t in tops]
    total = sum(f * t for f, t in zip(factors, totals))
    factors = jnp.concatenate([f / total for f in factors], axis=0)
    high = factors.astype(bf16)
    low = (factors - high.astype(f32)).astype(bf16)
    factors = dot(high, head_one) + dot(low, head_one)
    mixed = sum(
        factors[s * TOK_DEV : (s + 1) * TOK_DEV] * inbox[s, :, :C_TOK].astype(f32)
        for s in range(COLS)
    )
    gated = (mixed * jax.nn.sigmoid(gate_ref[...].astype(f32))).astype(bf16)
    token_out = (state_ref[...] + dot(gated, w_tok_out_ref[...])).astype(bf16)
    token_out_ref[...] = token_out
    count = count_ref[0]
    member = membership(token_ref[...], count, block).astype(bf16)
    same = (iota((CAP, CAP), 0) == iota((CAP, CAP), 1)).astype(bf16)
    chosen = dot(dot_nt(same, member).astype(bf16), token_out).astype(bf16)
    back = mid_ref[...].astype(f32) + dot(chosen, w_back_ref[...])
    atom_out_ref[...] = jnp.where(iota((CAP, 1), 0) < count, back, 0.0).astype(bf16)
    write.wait()


def finish_part(count, pair, inbox, gate, state, mid, token, w_tok_out, w_back):
    return pl.pallas_call(
        finish_kernel,
        out_shape=[
            jax.ShapeDtypeStruct((TOK_DEV, C_TOK), bf16),
            jax.ShapeDtypeStruct((CAP, C_ATOM), bf16),
            jax.ShapeDtypeStruct(pair.shape, bf16),
        ],
        in_specs=[SMEM, ANY] + [VMEM] * 7,
        out_specs=[VMEM, VMEM, ANY],
        scratch_shapes=[pltpu.SemaphoreType.DMA],
        compiler_params=pltpu.CompilerParams(vmem_limit_bytes=16 << 20),
        name="finish_part",
    )(count, pair, inbox, gate, state, mid, token, w_tok_out, w_back)


def local(
    atom_feat,
    atom_token,
    atom_count,
    window_start,
    w_atom_qkv,
    w_atom_out,
    w_atom_tok,
    single,
    tok_gain,
    w_tok,
    w_tok_out,
    pair,
    w_pair_in,
    w_pair_out,
    w_bias,
    w_back,
):
    token = atom_token.reshape(1, CAP)
    sides = (
        window_start, atom_feat, token, w_atom_qkv, w_atom_out, w_atom_tok, single, tok_gain, w_tok,
        pair, w_pair_in, w_pair_out, w_bias.T,
    )
    sides = [pltpu.with_memory_space_constraint(array, pltpu.HBM) for array in sides]
    pair_new, inbox, mid, state, gate = main_part(atom_count, *sides)
    return tuple(
        finish_part(atom_count, pair_new, inbox, gate, state, mid, token, w_tok_out, w_back)
    )


def solution(mesh):
    tokens = P(("row", "col"), None)
    flat = P(("row", "col"))
    return jax.shard_map(
        local,
        mesh=mesh,
        in_specs=(
            tokens, flat, flat, flat, P(), P(), P(), tokens, P(), P(), P(), P("row", "col", None),
            P(), P(), P(), P(),
        ),
        out_specs=(tokens, tokens, P("row", "col", None)),
        check_vma=False,
    )
```

```python
import functools
import math

import jax
import jax.numpy as jnp
from jax import lax
from jax.experimental import pallas as pl
from jax.experimental.pallas import tpu as pltpu
from jax.sharding import PartitionSpec as P

ATOM_HEADS = 4
TOK_HEADS = 16
QUERY_BLOCK = 32
KEY_WINDOW = 128
BEFORE = KEY_WINDOW // 2
AFTER = KEY_WINDOW - QUERY_BLOCK
CAP = 256
TOK_DEV = 16
C_ATOM = 128
C_TOK = 768
C_PAIR = 128
HID = 256
ROWS = 8
COLS = 16
TILE_I = 256
TILE_J = 128
MESSAGE = C_TOK + 128
EPS = 1e-05

f32 = jnp.float32
bf16 = jnp.bfloat16
MESH = pl.DeviceIdType.MESH
VMEM = pl.BlockSpec(memory_space=pltpu.VMEM)
SMEM = pl.BlockSpec(memory_space=pltpu.SMEM)
ANY = pl.BlockSpec(memory_space=pl.ANY)
HBM = pl.BlockSpec(memory_space=pltpu.HBM)


def dot(a, b):
    return jnp.dot(a, b, preferred_element_type=f32)


def dot_nt(a, b):
    return lax.dot_general(a, b, (((1,), (1,)), ((), ())), preferred_element_type=f32)


def iota(shape, dim):
    return lax.broadcasted_iota(jnp.int32, shape, dim)


def membership(token, live_count, block):
    shape = (TOK_DEV, CAP)
    local = token - block * TOK_DEV
    return ((iota(shape, 0) == local) & (iota(shape, 1) < live_count)).astype(f32)


CHUNK = 32
CHUNKS = TILE_I // CHUNK
EARLY = 1
PAIRED = 6
SCHEDULE = ((0, 5), (1, 2), (1, 1))
WINDOWS = (0, 128, 384, 512)
WIDE = 256
GROUP = 4


def atom_attention(block, count, starts_ref, feat, tail, head, w_qkv_ref, w_out_ref):
    last = ROWS * COLS - 1
    rows = jnp.concatenate([tail, feat, head], axis=0)
    length = rows.shape[0]
    queries = dot(feat, w_qkv_ref[:, :C_ATOM]).astype(bf16)
    keys_values = dot(rows, w_qkv_ref[:, C_ATOM:]).astype(bf16)
    keys, values = keys_values[:, :C_ATOM], keys_values[:, C_ATOM:]
    index = iota((1, length), 1)
    absent = -(1 << 20)
    shift_tail = jnp.where(block > 0, 0, absent)
    shift_head = jnp.where(block < last, count - CAP, absent)
    shift_own = jnp.where(index < BEFORE + count, 0, absent)
    position = index + jnp.where(
        index < BEFORE, shift_tail, jnp.where(index < BEFORE + CAP, shift_own, shift_head)
    )
    window = iota((CAP, 1), 0) // QUERY_BLOCK
    start = jnp.zeros((CAP, 1), jnp.int32)
    for b in range(CAP // QUERY_BLOCK):
        start = jnp.where(window == b, starts_ref[b] + BEFORE, start)
    allowed = (position >= start) & (position < start + KEY_WINDOW)
    width = C_ATOM // ATOM_HEADS
    lane = iota((CAP, C_ATOM), 1)
    mixed = jnp.zeros((CAP, C_ATOM), f32)
    for h in range(ATOM_HEADS):
        mine = (lane >= h * width) & (lane < (h + 1) * width)
        scores = dot_nt(jnp.where(mine, queries, jnp.zeros_like(queries)), keys)
        scores = jnp.where(allowed, scores * (1.0 / math.sqrt(width)), -1e30)
        weights = jnp.exp(scores - jnp.max(scores, axis=1, keepdims=True))
        total = jnp.sum(weights, axis=1, keepdims=True)
        mixed = jnp.where(mine, dot(weights.astype(bf16), values) / total, mixed)
    return (feat.astype(f32) + dot(mixed.astype(bf16), w_out_ref[...])).astype(bf16)


def main_kernel(
    count_ref, starts_hbm, feat_hbm, token_hbm, w_qkv_hbm, w_out_hbm, w_lift_hbm, single_hbm, gain_hbm, w_tok_hbm,
    pair_hbm, w_in_hbm, w_pair_out_hbm, w_bias_hbm,
    done, inbox, mid_ref, state_ref, gate_ref,
    starts_ref, feat_ref, token_ref, w_qkv_ref, w_out_ref, w_lift_ref, single_ref, gain_ref, w_tok_ref, w_in_ref, w_pair_out_ref,
    w_bias_ref, load_sem, held, pair_sem, w_up, w_down, bias_ref, tail_out, tail_ref, head_ref, halo_send, halo_recv,
    query_ref, kv_ref, queries_ref, kvs_ref, q_send, q_recv, kv_send, kv_recv, outbox, out_send, out_recv,
):
    r, c = lax.axis_index("row"), lax.axis_index("col")
    block = r * COLS + c
    last = ROWS * COLS - 1
    count = count_ref[0]
    sides = [
        (feat_hbm, feat_ref), (w_in_hbm, w_in_ref), (w_pair_out_hbm, w_pair_out_ref), (w_bias_hbm, w_bias_ref),
        (w_qkv_hbm, w_qkv_ref), (w_out_hbm, w_out_ref), (w_lift_hbm, w_lift_ref), (token_hbm, token_ref),
        (single_hbm, single_ref), (starts_hbm, starts_ref), (gain_hbm, gain_ref), (w_tok_hbm, w_tok_ref),
    ]
    loads = [
        pltpu.make_async_copy(src, dst, load_sem.at[n]) for n, (src, dst) in enumerate(sides)
    ]

    def chunk_at(t):
        return lax.rem(c // 2 + 1 + t, CHUNKS)

    def pair_load(t):
        k = chunk_at(t)
        rows = pl.ds(k * CHUNK, CHUNK)
        return pltpu.make_async_copy(pair_hbm.at[rows], held.at[rows], pair_sem.at[k])

    for load in loads[:4]:
        load.start()
    pair_load(0).start()
    for load in loads[4:]:
        load.start()
    for t in range(1, CHUNKS):
        pair_load(t).start()

    barrier = pltpu.get_barrier_semaphore()

    def greet(row, col):
        pl.semaphore_signal(barrier, inc=1, device_id=(row, col), device_id_type=MESH)

    def beside(distance):
        other = block + distance
        return other // COLS, lax.rem(other, COLS)

    def kv_source(k):
        return c // 2, lax.rem(c, 2) * ROWS + k

    def kv_target(k):
        return k, 2 * r + c // ROWS

    kv_here = c == 2 * r + c // ROWS

    def elsewhere(device):
        return (device[0] != r) | (device[1] != c)

    @pl.when(block > 0)
    def _():
        greet(*beside(-1))

    @pl.when(block < last)
    def _():
        greet(*beside(1))

    for k in range(1, COLS):
        greet(r, lax.rem(c + k, COLS))
    for k in range(ROWS):

        @pl.when(elsewhere(kv_source(k)))
        def _():
            greet(*kv_source(k))

    heard = (block > 0).astype(jnp.int32) + (block < last).astype(jnp.int32)
    pl.semaphore_wait(barrier, COLS - 1 + ROWS - kv_here.astype(jnp.int32) + heard)

    loads[0].wait()
    pick = iota((BEFORE, CAP), 1) == iota((BEFORE, CAP), 0) + (count - BEFORE)
    tail_out[...] = dot(pick.astype(bf16), feat_ref[...]).astype(bf16)

    def halo_copy(n, src, dst, distance):
        return pltpu.make_async_remote_copy(
            src_ref=src,
            dst_ref=dst,
            send_sem=halo_send.at[n],
            recv_sem=halo_recv.at[n],
            device_id=beside(distance),
            device_id_type=MESH,
        )

    def tail_copy():
        return halo_copy(0, tail_out, tail_ref, 1)

    def head_copy():
        return halo_copy(1, feat_ref.at[pl.ds(0, AFTER)], head_ref, -1)

    @pl.when(block < last)
    def _():
        tail_copy().start()

    @pl.when(block > 0)
    def _():
        head_copy().start()

    @pl.when(block == 0)
    def _():
        tail_ref[...] = jnp.zeros_like(tail_ref)

    @pl.when(block == last)
    def _():
        head_ref[...] = jnp.zeros_like(head_ref)

    for load in loads[1:4]:
        load.wait()
    w_in = w_in_ref[...].astype(f32)
    w_up[:HID] = (w_in[:, :HID].T * 0.5).astype(bf16)
    w_up[HID : 2 * HID] = w_in[:, HID:].T.astype(bf16)
    w_up[2 * HID :] = w_bias_ref[...]
    w_down[:C_PAIR] = w_pair_out_ref[...].astype(f32).T.astype(bf16)
    w_bias = w_bias_ref[...].astype(f32)
    w_bias = w_bias - jnp.mean(w_bias, axis=1, keepdims=True)
    high = w_bias.astype(bf16)
    low = (w_bias - high.astype(f32)).astype(bf16)
    w_pair_out = w_pair_out_ref[...]
    w_down[C_PAIR:] = (dot_nt(high, w_pair_out) + dot_nt(low, w_pair_out)).astype(bf16)
    share = 1.0 / C_PAIR

    def pair_step(t):
        pair_load(t).wait()
        k = chunk_at(t)
        rows = pl.ds(k * CHUNK, CHUNK)
        tile = held[rows].reshape(CHUNK * TILE_J, C_PAIR).T
        wide = tile.astype(f32)
        mean = jnp.sum(wide, axis=0, keepdims=True) * share
        centred = wide - mean
        spread = jnp.sum(centred * centred, axis=0, keepdims=True) * share + EPS
        scale = lax.rsqrt(spread)
        up = dot(w_up[...], (centred * scale).astype(bf16))
        gate, value = up[:HID].astype(bf16), up[HID : 2 * HID].astype(bf16)
        hidden = (gate + gate * jnp.tanh(gate)) * value
        down = dot(w_down[...], hidden)
        moved = centred + down[:C_PAIR]
        done[rows] = (moved + mean).astype(bf16).T.reshape(CHUNK, TILE_J, C_PAIR)
        moved_mean = jnp.sum(moved, axis=0, keepdims=True) * share
        spread_again = jnp.sum(moved * moved, axis=0, keepdims=True) * share
        spread_again = jnp.maximum(spread_again - moved_mean * moved_mean, 0.0) + EPS
        bias = up[2 * HID :] * (spread * scale) + down[C_PAIR:]
        bias = bias * lax.rsqrt(spread_again)
        bias_ref[t] = bias.reshape(TOK_HEADS * CHUNK, TILE_J)

    def loop(first, stop, step):
        if stop == first + 1:
            step(first)
        if stop <= first + 1:
            return

        def body(t, carry):
            step(t)
            return carry

        lax.fori_loop(first, stop, body, 0)

    loop(0, EARLY, pair_step)

    @pl.when(block > 0)
    def _():
        halo_copy(0, tail_out, tail_ref, -1).wait_recv()
        head_copy().wait_send()

    @pl.when(block < last)
    def _():
        halo_copy(1, feat_ref.at[pl.ds(0, AFTER)], head_ref, 1).wait_recv()
        tail_copy().wait_send()

    for load in loads[4:]:
        load.wait()
    mid = atom_attention(
        block, count, starts_ref, feat_ref[...], tail_ref[...], head_ref[...], w_qkv_ref, w_out_ref
    )
    mid_ref[...] = mid
    lifted = jnp.maximum(dot(mid, w_lift_ref[...]), 0.0).astype(bf16)
    member = membership(token_ref[...], count, block)
    members = jnp.sum(member, axis=1, keepdims=True)
    state = single_ref[...].astype(f32) + dot(member.astype(bf16), lifted) / members
    state_ref[...] = state
    centred = state - jnp.mean(state, axis=1, keepdims=True)
    spread = jnp.mean(centred * centred, axis=1, keepdims=True)
    normed = (centred * lax.rsqrt(spread + EPS) * gain_ref[...].reshape(1, C_TOK)).astype(bf16)
    kv_ref[...] = dot(normed, w_tok_ref[:, C_TOK : 3 * C_TOK]).astype(bf16)

    def kv_copy(k):
        slot = lax.rem(c, ROWS)
        return pltpu.make_async_remote_copy(
            src_ref=kv_ref,
            dst_ref=kvs_ref.at[slot],
            send_sem=kv_send.at[k],
            recv_sem=kv_recv.at[slot],
            device_id=kv_target(k),
            device_id_type=MESH,
        )

    def kv_arrival(k):
        return pltpu.make_async_remote_copy(
            src_ref=kv_ref,
            dst_ref=kvs_ref.at[k],
            send_sem=kv_send.at[k],
            recv_sem=kv_recv.at[k],
            device_id=kv_source(k),
            device_id_type=MESH,
        )

    def q_copy(k):
        return pltpu.make_async_remote_copy(
            src_ref=query_ref,
            dst_ref=queries_ref.at[c],
            send_sem=q_send.at[k],
            recv_sem=q_recv.at[c],
            device_id=(r, lax.rem(c + k, COLS)),
            device_id_type=MESH,
        )

    def q_arrival(k):
        s = lax.rem(c + k, COLS)
        return pltpu.make_async_remote_copy(
            src_ref=query_ref,
            dst_ref=queries_ref.at[s],
            send_sem=q_send.at[k],
            recv_sem=q_recv.at[s],
            device_id=(r, s),
            device_id_type=MESH,
        )

    for k in range(ROWS):

        @pl.when(elsewhere(kv_target(k)))
        def _():
            kv_copy(k).start()

    query_ref[...] = dot(normed, w_tok_ref[:, :C_TOK]).astype(bf16)
    for k in range(1, COLS):
        q_copy(k).start()
    gate_ref[...] = dot(normed, w_tok_ref[:, 3 * C_TOK :]).astype(bf16)
    queries_ref[c] = query_ref[...]

    @pl.when(kv_here)
    def _():
        kvs_ref[lax.rem(c, ROWS)] = kv_ref[...]

    loop(EARLY, PAIRED, pair_step)

    for k in range(ROWS):

        @pl.when(elsewhere(kv_source(k)))
        def _():
            kv_arrival(k).wait_recv()

        @pl.when(elsewhere(kv_target(k)))
        def _():
            kv_copy(k).wait_send()

    for k in range(1, COLS):
        q_arrival(k).wait_recv()
        q_copy(k).wait_send()

    width = C_TOK // TOK_HEADS
    kvs = kvs_ref[...].reshape(TILE_J, 2 * C_TOK)
    column = iota((CHUNK, WIDE), 1)
    lane = iota((CHUNK, 128), 1)

    def out_copy(to):
        return pltpu.make_async_remote_copy(
            src_ref=outbox.at[to],
            dst_ref=inbox.at[c],
            send_sem=out_send.at[to],
            recv_sem=out_recv.at[c],
            device_id=(r, to),
            device_id_type=MESH,
        )

    def out_arrival(s):
        return pltpu.make_async_remote_copy(
            src_ref=outbox.at[s],
            dst_ref=inbox.at[s],
            send_sem=out_send.at[s],
            recv_sem=out_recv.at[s],
            device_id=(r, s),
            device_id_type=MESH,
        )

    def attend(first, chunks):
        places = [chunk_at(first + n) for n in range(chunks)]
        queries = [queries_ref[pl.ds(2 * k, 2)].reshape(CHUNK, C_TOK) for k in places]
        parts = [[] for _ in places]
        notes = [jnp.zeros((CHUNK, 128), f32) for _ in places]
        for g, at in enumerate(WINDOWS):
            heads = range(GROUP * g, GROUP * (g + 1))
            mine = [(column >= h * width - at) & (column < (h + 1) * width - at) for h in heads]
            stack = []
            for q in queries:
                seen = q[:, at : at + WIDE]
                stack += [jnp.where(m, seen, jnp.zeros_like(seen)) for m in mine]
            scores = dot_nt(jnp.concatenate(stack, axis=0), kvs[:, at : at + WIDE])
            bias = bias_ref[pl.ds(first, chunks), pl.ds(g * GROUP * CHUNK, GROUP * CHUNK), :]
            scores = scores * (1.0 / math.sqrt(width)) + bias.reshape(scores.shape)
            top = jnp.max(scores, axis=1, keepdims=True).astype(bf16).astype(f32)
            weights = jnp.exp(scores - top)
            total = jnp.sum(weights, axis=1, keepdims=True)
            mixed = dot(weights.astype(bf16), kvs[:, C_TOK + at : C_TOK + at + WIDE])
            for n in range(chunks):
                part = jnp.zeros((CHUNK, WIDE), f32)
                for i, (h, m) in enumerate(zip(heads, mine)):
                    rows = slice((n * GROUP + i) * CHUNK, (n * GROUP + i + 1) * CHUNK)
                    part = jnp.where(m, mixed[rows], part)
                    high = total[rows].astype(bf16).astype(f32)
                    note = jnp.where(lane == h, top[rows], notes[n])
                    note = jnp.where(lane == TOK_HEADS + h, high, note)
                    notes[n] = jnp.where(lane == 2 * TOK_HEADS + h, total[rows] - high, note)
                parts[n].append(part)
        half = WIDE // 2
        for k, (a, b, d, e), note in zip(places, parts, notes):
            message = [
                a[:, :half], a[:, half:] + b[:, :half], b[:, half:],
                d[:, :half], d[:, half:] + e[:, :half], e[:, half:], note,
            ]
            message = jnp.concatenate(message, axis=1).astype(bf16)
            outbox[pl.ds(2 * k, 2)] = message.reshape(2, TOK_DEV, MESSAGE)
            for n in range(2):

                @pl.when(2 * k + n != c)
                def _():
                    out_copy(2 * k + n).start()

    paired, attended = PAIRED, 0
    for pairs, chunks in SCHEDULE:
        loop(paired, paired + pairs, pair_step)
        attend(attended, chunks)
        paired, attended = paired + pairs, attended + chunks
    inbox[c] = outbox[c]

    def arrived(k):
        s = lax.rem(c + k, COLS)
        out_arrival(s).wait_recv()
        out_copy(s).wait_send()

    loop(1, COLS, arrived)


def main_part(count, starts, feat, token, w_qkv, w_out, w_lift, single, gain, w_tok, pair, w_in, w_pair_out, w_bias):
    def vmem(*shape):
        return pltpu.VMEM(shape, bf16)

    def dma(n):
        return pltpu.SemaphoreType.DMA((n,))

    return pl.pallas_call(
        main_kernel,
        out_shape=[
            jax.ShapeDtypeStruct((TILE_I, TILE_J, C_PAIR), bf16),
            jax.ShapeDtypeStruct((COLS, TOK_DEV, MESSAGE), bf16),
            jax.ShapeDtypeStruct((CAP, C_ATOM), bf16),
            jax.ShapeDtypeStruct((TOK_DEV, C_TOK), f32),
            jax.ShapeDtypeStruct((TOK_DEV, C_TOK), bf16),
        ],
        in_specs=[SMEM] + [HBM] * 13,
        out_specs=[VMEM] * 5,
        scratch_shapes=[
            pltpu.SMEM((CAP // QUERY_BLOCK,), jnp.int32), vmem(CAP, C_ATOM), pltpu.VMEM((1, CAP), jnp.int32),
            vmem(C_ATOM, 3 * C_ATOM), vmem(C_ATOM, C_ATOM), vmem(C_ATOM, C_TOK), vmem(TOK_DEV, C_TOK),
            pltpu.VMEM((C_TOK,), f32), vmem(C_TOK, 4 * C_TOK), vmem(C_PAIR, 2 * HID), vmem(HID, C_PAIR),
            vmem(TOK_HEADS, C_PAIR), dma(12),
            vmem(TILE_I, TILE_J, C_PAIR), dma(CHUNKS),
            vmem(2 * HID + TOK_HEADS, C_PAIR), vmem(C_PAIR + TOK_HEADS, HID),
            pltpu.VMEM((CHUNKS, TOK_HEADS * CHUNK, TILE_J), f32),
            vmem(BEFORE, C_ATOM), vmem(BEFORE, C_ATOM), vmem(AFTER, C_ATOM), dma(2), dma(2),
            vmem(TOK_DEV, C_TOK), vmem(TOK_DEV, 2 * C_TOK),
            vmem(COLS, TOK_DEV, C_TOK), vmem(ROWS, TOK_DEV, 2 * C_TOK),
            dma(COLS), dma(COLS), dma(ROWS), dma(ROWS),
            vmem(COLS, TOK_DEV, MESSAGE), dma(COLS), dma(COLS),
        ],
        compiler_params=pltpu.CompilerParams(
            collective_id=0, has_side_effects=True, vmem_limit_bytes=36 << 20
        ),
        name="main_part",
    )(count, starts, feat, token, w_qkv, w_out, w_lift, single, gain, w_tok, pair, w_in, w_pair_out, w_bias)


def finish_kernel(
    count_ref, pair_ref, inbox, gate_ref, state_ref, mid_ref, token_ref, w_tok_out_ref, w_back_ref,
    token_out_ref, atom_out_ref, pair_out_ref, sem,
):
    write = pltpu.make_async_copy(pair_ref, pair_out_ref, sem)
    write.start()
    block = lax.axis_index("row") * COLS + lax.axis_index("col")
    width = C_TOK // TOK_HEADS
    head = iota((TOK_HEADS, C_TOK), 0) * width
    column = iota((TOK_HEADS, C_TOK), 1)
    head_one = ((column >= head) & (column < head + width)).astype(bf16)
    n = TOK_HEADS
    tails = [inbox[s, :, C_TOK:].astype(f32) for s in range(COLS)]
    tops = [t[:, :n] for t in tails]
    totals = [t[:, n : 2 * n] + t[:, 2 * n : 3 * n] for t in tails]
    top = functools.reduce(jnp.maximum, tops)
    factors = [jnp.exp(t - top) for t in tops]
    total = sum(f * t for f, t in zip(factors, totals))
    factors = jnp.concatenate([f / total for f in factors], axis=0)
    high = factors.astype(bf16)
    low = (factors - high.astype(f32)).astype(bf16)
    factors = dot(high, head_one) + dot(low, head_one)
    mixed = sum(
        factors[s * TOK_DEV : (s + 1) * TOK_DEV] * inbox[s, :, :C_TOK].astype(f32)
        for s in range(COLS)
    )
    gated = (mixed * jax.nn.sigmoid(gate_ref[...].astype(f32))).astype(bf16)
    token_out = (state_ref[...] + dot(gated, w_tok_out_ref[...])).astype(bf16)
    token_out_ref[...] = token_out
    count = count_ref[0]
    member = membership(token_ref[...], count, block).astype(bf16)
    same = (iota((CAP, CAP), 0) == iota((CAP, CAP), 1)).astype(bf16)
    chosen = dot(dot_nt(same, member).astype(bf16), token_out).astype(bf16)
    back = mid_ref[...].astype(f32) + dot(chosen, w_back_ref[...])
    atom_out_ref[...] = jnp.where(iota((CAP, 1), 0) < count, back, 0.0).astype(bf16)
    write.wait()


def finish_part(count, pair, inbox, gate, state, mid, token, w_tok_out, w_back):
    return pl.pallas_call(
        finish_kernel,
        out_shape=[
            jax.ShapeDtypeStruct((TOK_DEV, C_TOK), bf16),
            jax.ShapeDtypeStruct((CAP, C_ATOM), bf16),
            jax.ShapeDtypeStruct(pair.shape, bf16),
        ],
        in_specs=[SMEM, ANY] + [VMEM] * 7,
        out_specs=[VMEM, VMEM, ANY],
        scratch_shapes=[pltpu.SemaphoreType.DMA],
        compiler_params=pltpu.CompilerParams(vmem_limit_bytes=16 << 20),
        name="finish_part",
    )(count, pair, inbox, gate, state, mid, token, w_tok_out, w_back)


def local(
    atom_feat,
    atom_token,
    atom_count,
    window_start,
    w_atom_qkv,
    w_atom_out,
    w_atom_tok,
    single,
    tok_gain,
    w_tok,
    w_tok_out,
    pair,
    w_pair_in,
    w_pair_out,
    w_bias,
    w_back,
):
    token = atom_token.reshape(1, CAP)
    sides = (
        window_start, atom_feat, token, w_atom_qkv, w_atom_out, w_atom_tok, single, tok_gain, w_tok,
        pair, w_pair_in, w_pair_out, w_bias.T,
    )
    sides = [pltpu.with_memory_space_constraint(array, pltpu.HBM) for array in sides]
    pair_new, inbox, mid, state, gate = main_part(atom_count, *sides)
    return tuple(
        finish_part(atom_count, pair_new, inbox, gate, state, mid, token, w_tok_out, w_back)
    )


def solution(mesh):
    tokens = P(("row", "col"), None)
    flat = P(("row", "col"))
    return jax.shard_map(
        local,
        mesh=mesh,
        in_specs=(
            tokens, flat, flat, flat, P(), P(), P(), tokens, P(), P(), P(), P("row", "col", None),
            P(), P(), P(), P(),
        ),
        out_specs=(tokens, tokens, P("row", "col", None)),
        check_vma=False,
    )
```

```python
import functools
import math

import jax
import jax.numpy as jnp
from jax import lax
from jax.experimental import pallas as pl
from jax.experimental.pallas import tpu as pltpu
from jax.sharding import PartitionSpec as P

ATOM_HEADS = 4
TOK_HEADS = 16
QUERY_BLOCK = 32
KEY_WINDOW = 128
BEFORE = KEY_WINDOW // 2
AFTER = KEY_WINDOW - QUERY_BLOCK
CAP = 256
TOK_DEV = 16
C_ATOM = 128
C_TOK = 768
C_PAIR = 128
HID = 256
ROWS = 8
COLS = 16
TILE_I = 256
TILE_J = 128
MESSAGE = C_TOK + 128
EPS = 1e-05

f32 = jnp.float32
bf16 = jnp.bfloat16
MESH = pl.DeviceIdType.MESH
VMEM = pl.BlockSpec(memory_space=pltpu.VMEM)
SMEM = pl.BlockSpec(memory_space=pltpu.SMEM)
ANY = pl.BlockSpec(memory_space=pl.ANY)
HBM = pl.BlockSpec(memory_space=pltpu.HBM)


def dot(a, b):
    return jnp.dot(a, b, preferred_element_type=f32)


def dot_nt(a, b):
    return lax.dot_general(a, b, (((1,), (1,)), ((), ())), preferred_element_type=f32)


def iota(shape, dim):
    return lax.broadcasted_iota(jnp.int32, shape, dim)


def membership(token, live_count, block):
    shape = (TOK_DEV, CAP)
    local = token - block * TOK_DEV
    return ((iota(shape, 0) == local) & (iota(shape, 1) < live_count)).astype(f32)


CHUNK = 32
CHUNKS = TILE_I // CHUNK
EARLY = 2
PAIRED = 6
SCHEDULE = ((0, 5), (1, 2), (1, 1))
WINDOWS = (0, 128, 384, 512)
WIDE = 256
GROUP = 4


def atom_attention(block, count, starts_ref, feat, tail, head, w_qkv_ref, w_out_ref):
    last = ROWS * COLS - 1
    rows = jnp.concatenate([tail, feat, head], axis=0)
    length = rows.shape[0]
    queries = dot(feat, w_qkv_ref[:, :C_ATOM]).astype(bf16)
    keys_values = dot(rows, w_qkv_ref[:, C_ATOM:]).astype(bf16)
    keys, values = keys_values[:, :C_ATOM], keys_values[:, C_ATOM:]
    index = iota((1, length), 1)
    absent = -(1 << 20)
    shift_tail = jnp.where(block > 0, 0, absent)
    shift_head = jnp.where(block < last, count - CAP, absent)
    shift_own = jnp.where(index < BEFORE + count, 0, absent)
    position = index + jnp.where(
        index < BEFORE, shift_tail, jnp.where(index < BEFORE + CAP, shift_own, shift_head)
    )
    window = iota((CAP, 1), 0) // QUERY_BLOCK
    start = jnp.zeros((CAP, 1), jnp.int32)
    for b in range(CAP // QUERY_BLOCK):
        start = jnp.where(window == b, starts_ref[b] + BEFORE, start)
    allowed = (position >= start) & (position < start + KEY_WINDOW)
    width = C_ATOM // ATOM_HEADS
    lane = iota((CAP, C_ATOM), 1)
    mixed = jnp.zeros((CAP, C_ATOM), f32)
    for h in range(ATOM_HEADS):
        mine = (lane >= h * width) & (lane < (h + 1) * width)
        scores = dot_nt(jnp.where(mine, queries, jnp.zeros_like(queries)), keys)
        scores = jnp.where(allowed, scores * (1.0 / math.sqrt(width)), -1e30)
        weights = jnp.exp(scores - jnp.max(scores, axis=1, keepdims=True))
        total = jnp.sum(weights, axis=1, keepdims=True)
        mixed = jnp.where(mine, dot(weights.astype(bf16), values) / total, mixed)
    return (feat.astype(f32) + dot(mixed.astype(bf16), w_out_ref[...])).astype(bf16)


def main_kernel(
    count_ref, starts_hbm, feat_hbm, token_hbm, w_qkv_hbm, w_out_hbm, w_lift_hbm, single_hbm, gain_hbm, w_tok_hbm,
    pair_hbm, w_in_hbm, w_pair_out_hbm, w_bias_hbm,
    done, inbox, mid_ref, state_ref, gate_ref,
    starts_ref, feat_ref, token_ref, w_qkv_ref, w_out_ref, w_lift_ref, single_ref, gain_ref, w_tok_ref, w_in_ref, w_pair_out_ref,
    w_bias_ref, load_sem, held, pair_sem, w_up, w_down, bias_ref, tail_out, tail_ref, head_ref, halo_send, halo_recv,
    query_ref, kv_ref, queries_ref, kvs_ref, q_send, q_recv, kv_send, kv_recv, outbox, out_send, out_recv,
):
    r, c = lax.axis_index("row"), lax.axis_index("col")
    block = r * COLS + c
    last = ROWS * COLS - 1
    count = count_ref[0]
    sides = [
        (feat_hbm, feat_ref), (w_in_hbm, w_in_ref), (w_pair_out_hbm, w_pair_out_ref), (w_bias_hbm, w_bias_ref),
        (w_qkv_hbm, w_qkv_ref), (w_out_hbm, w_out_ref), (w_lift_hbm, w_lift_ref), (token_hbm, token_ref),
        (single_hbm, single_ref), (starts_hbm, starts_ref), (gain_hbm, gain_ref), (w_tok_hbm, w_tok_ref),
    ]
    loads = [
        pltpu.make_async_copy(src, dst, load_sem.at[n]) for n, (src, dst) in enumerate(sides)
    ]

    def chunk_at(t):
        return lax.rem(c // 2 + 1 + t, CHUNKS)

    def pair_load(t):
        k = chunk_at(t)
        rows = pl.ds(k * CHUNK, CHUNK)
        return pltpu.make_async_copy(pair_hbm.at[rows], held.at[rows], pair_sem.at[k])

    for load in loads[:4]:
        load.start()
    pair_load(0).start()
    for load in loads[4:]:
        load.start()
    for t in range(1, CHUNKS):
        pair_load(t).start()

    barrier = pltpu.get_barrier_semaphore()

    def greet(row, col):
        pl.semaphore_signal(barrier, inc=1, device_id=(row, col), device_id_type=MESH)

    def beside(distance):
        other = block + distance
        return other // COLS, lax.rem(other, COLS)

    def kv_source(k):
        return c // 2, lax.rem(c, 2) * ROWS + k

    def kv_target(k):
        return k, 2 * r + c // ROWS

    kv_here = c == 2 * r + c // ROWS

    def elsewhere(device):
        return (device[0] != r) | (device[1] != c)

    @pl.when(block > 0)
    def _():
        greet(*beside(-1))

    @pl.when(block < last)
    def _():
        greet(*beside(1))

    for k in range(1, COLS):
        greet(r, lax.rem(c + k, COLS))
    for k in range(ROWS):

        @pl.when(elsewhere(kv_source(k)))
        def _():
            greet(*kv_source(k))

    loads[0].wait()
    pick = iota((BEFORE, CAP), 1) == iota((BEFORE, CAP), 0) + (count - BEFORE)
    tail_out[...] = dot(pick.astype(bf16), feat_ref[...]).astype(bf16)

    for load in loads[1:4]:
        load.wait()
    w_in = w_in_ref[...].astype(f32)
    w_up[:HID] = (w_in[:, :HID].T * 0.5).astype(bf16)
    w_up[HID : 2 * HID] = w_in[:, HID:].T.astype(bf16)
    w_up[2 * HID :] = w_bias_ref[...]
    w_down[:C_PAIR] = w_pair_out_ref[...].astype(f32).T.astype(bf16)
    w_bias = w_bias_ref[...].astype(f32)
    w_bias = w_bias - jnp.mean(w_bias, axis=1, keepdims=True)
    high = w_bias.astype(bf16)
    low = (w_bias - high.astype(f32)).astype(bf16)
    w_pair_out = w_pair_out_ref[...]
    w_down[C_PAIR:] = (dot_nt(high, w_pair_out) + dot_nt(low, w_pair_out)).astype(bf16)
    share = 1.0 / C_PAIR

    def pair_step(t):
        pair_load(t).wait()
        k = chunk_at(t)
        rows = pl.ds(k * CHUNK, CHUNK)
        tile = held[rows].reshape(CHUNK * TILE_J, C_PAIR).T
        wide = tile.astype(f32)
        mean = jnp.sum(wide, axis=0, keepdims=True) * share
        centred = wide - mean
        spread = jnp.sum(centred * centred, axis=0, keepdims=True) * share + EPS
        scale = lax.rsqrt(spread)
        up = dot(w_up[...], (centred * scale).astype(bf16))
        gate, value = up[:HID].astype(bf16), up[HID : 2 * HID].astype(bf16)
        hidden = (gate + gate * jnp.tanh(gate)) * value
        down = dot(w_down[...], hidden)
        moved = centred + down[:C_PAIR]
        done[rows] = (moved + mean).astype(bf16).T.reshape(CHUNK, TILE_J, C_PAIR)
        moved_mean = jnp.sum(moved, axis=0, keepdims=True) * share
        spread_again = jnp.sum(moved * moved, axis=0, keepdims=True) * share
        spread_again = jnp.maximum(spread_again - moved_mean * moved_mean, 0.0) + EPS
        bias = up[2 * HID :] * (spread * scale) + down[C_PAIR:]
        bias = bias * lax.rsqrt(spread_again)
        bias_ref[t] = bias.reshape(TOK_HEADS * CHUNK, TILE_J)

    def loop(first, stop, step):
        if stop == first + 1:
            step(first)
        if stop <= first + 1:
            return

        def body(t, carry):
            step(t)
            return carry

        lax.fori_loop(first, stop, body, 0)

    loop(0, 1, pair_step)
    heard = (block > 0).astype(jnp.int32) + (block < last).astype(jnp.int32)
    pl.semaphore_wait(barrier, COLS - 1 + ROWS - kv_here.astype(jnp.int32) + heard)

    def halo_copy(n, src, dst, distance):
        return pltpu.make_async_remote_copy(
            src_ref=src,
            dst_ref=dst,
            send_sem=halo_send.at[n],
            recv_sem=halo_recv.at[n],
            device_id=beside(distance),
            device_id_type=MESH,
        )

    def tail_copy():
        return halo_copy(0, tail_out, tail_ref, 1)

    def head_copy():
        return halo_copy(1, feat_ref.at[pl.ds(0, AFTER)], head_ref, -1)

    @pl.when(block < last)
    def _():
        tail_copy().start()

    @pl.when(block > 0)
    def _():
        head_copy().start()

    @pl.when(block == 0)
    def _():
        tail_ref[...] = jnp.zeros_like(tail_ref)

    @pl.when(block == last)
    def _():
        head_ref[...] = jnp.zeros_like(head_ref)

    loop(1, EARLY, pair_step)

    @pl.when(block > 0)
    def _():
        halo_copy(0, tail_out, tail_ref, -1).wait_recv()
        head_copy().wait_send()

    @pl.when(block < last)
    def _():
        halo_copy(1, feat_ref.at[pl.ds(0, AFTER)], head_ref, 1).wait_recv()
        tail_copy().wait_send()

    for load in loads[4:]:
        load.wait()
    mid = atom_attention(
        block, count, starts_ref, feat_ref[...], tail_ref[...], head_ref[...], w_qkv_ref, w_out_ref
    )
    mid_ref[...] = mid
    lifted = jnp.maximum(dot(mid, w_lift_ref[...]), 0.0).astype(bf16)
    member = membership(token_ref[...], count, block)
    members = jnp.sum(member, axis=1, keepdims=True)
    state = single_ref[...].astype(f32) + dot(member.astype(bf16), lifted) / members
    state_ref[...] = state
    centred = state - jnp.mean(state, axis=1, keepdims=True)
    spread = jnp.mean(centred * centred, axis=1, keepdims=True)
    normed = (centred * lax.rsqrt(spread + EPS) * gain_ref[...].reshape(1, C_TOK)).astype(bf16)
    kv_ref[...] = dot(normed, w_tok_ref[:, C_TOK : 3 * C_TOK]).astype(bf16)

    def kv_copy(k):
        slot = lax.rem(c, ROWS)
        return pltpu.make_async_remote_copy(
            src_ref=kv_ref,
            dst_ref=kvs_ref.at[slot],
            send_sem=kv_send.at[k],
            recv_sem=kv_recv.at[slot],
            device_id=kv_target(k),
            device_id_type=MESH,
        )

    def kv_arrival(k):
        return pltpu.make_async_remote_copy(
            src_ref=kv_ref,
            dst_ref=kvs_ref.at[k],
            send_sem=kv_send.at[k],
            recv_sem=kv_recv.at[k],
            device_id=kv_source(k),
            device_id_type=MESH,
        )

    def q_copy(k):
        return pltpu.make_async_remote_copy(
            src_ref=query_ref,
            dst_ref=queries_ref.at[c],
            send_sem=q_send.at[k],
            recv_sem=q_recv.at[c],
            device_id=(r, lax.rem(c + k, COLS)),
            device_id_type=MESH,
        )

    def q_arrival(k):
        s = lax.rem(c + k, COLS)
        return pltpu.make_async_remote_copy(
            src_ref=query_ref,
            dst_ref=queries_ref.at[s],
            send_sem=q_send.at[k],
            recv_sem=q_recv.at[s],
            device_id=(r, s),
            device_id_type=MESH,
        )

    for k in range(ROWS):

        @pl.when(elsewhere(kv_target(k)))
        def _():
            kv_copy(k).start()

    query_ref[...] = dot(normed, w_tok_ref[:, :C_TOK]).astype(bf16)
    for k in range(1, COLS):
        q_copy(k).start()
    gate_ref[...] = dot(normed, w_tok_ref[:, 3 * C_TOK :]).astype(bf16)
    queries_ref[c] = query_ref[...]

    @pl.when(kv_here)
    def _():
        kvs_ref[lax.rem(c, ROWS)] = kv_ref[...]

    loop(EARLY, PAIRED, pair_step)

    for k in range(ROWS):

        @pl.when(elsewhere(kv_source(k)))
        def _():
            kv_arrival(k).wait_recv()

        @pl.when(elsewhere(kv_target(k)))
        def _():
            kv_copy(k).wait_send()

    for k in range(1, COLS):
        q_arrival(k).wait_recv()
        q_copy(k).wait_send()

    width = C_TOK // TOK_HEADS
    kvs = kvs_ref[...].reshape(TILE_J, 2 * C_TOK)
    column = iota((CHUNK, WIDE), 1)
    lane = iota((CHUNK, 128), 1)

    def out_copy(to):
        return pltpu.make_async_remote_copy(
            src_ref=outbox.at[to],
            dst_ref=inbox.at[c],
            send_sem=out_send.at[to],
            recv_sem=out_recv.at[c],
            device_id=(r, to),
            device_id_type=MESH,
        )

    def out_arrival(s):
        return pltpu.make_async_remote_copy(
            src_ref=outbox.at[s],
            dst_ref=inbox.at[s],
            send_sem=out_send.at[s],
            recv_sem=out_recv.at[s],
            device_id=(r, s),
            device_id_type=MESH,
        )

    def attend(first, chunks):
        places = [chunk_at(first + n) for n in range(chunks)]
        queries = [queries_ref[pl.ds(2 * k, 2)].reshape(CHUNK, C_TOK) for k in places]
        parts = [[] for _ in places]
        notes = [jnp.zeros((CHUNK, 128), f32) for _ in places]
        for g, at in enumerate(WINDOWS):
            heads = range(GROUP * g, GROUP * (g + 1))
            mine = [(column >= h * width - at) & (column < (h + 1) * width - at) for h in heads]
            stack = []
            for q in queries:
                seen = q[:, at : at + WIDE]
                stack += [jnp.where(m, seen, jnp.zeros_like(seen)) for m in mine]
            scores = dot_nt(jnp.concatenate(stack, axis=0), kvs[:, at : at + WIDE])
            bias = bias_ref[pl.ds(first, chunks), pl.ds(g * GROUP * CHUNK, GROUP * CHUNK), :]
            scores = scores * (1.0 / math.sqrt(width)) + bias.reshape(scores.shape)
            top = jnp.max(scores, axis=1, keepdims=True).astype(bf16).astype(f32)
            weights = jnp.exp(scores - top)
            total = jnp.sum(weights, axis=1, keepdims=True)
            mixed = dot(weights.astype(bf16), kvs[:, C_TOK + at : C_TOK + at + WIDE])
            for n in range(chunks):
                part = jnp.zeros((CHUNK, WIDE), f32)
                for i, (h, m) in enumerate(zip(heads, mine)):
                    rows = slice((n * GROUP + i) * CHUNK, (n * GROUP + i + 1) * CHUNK)
                    part = jnp.where(m, mixed[rows], part)
                    high = total[rows].astype(bf16).astype(f32)
                    note = jnp.where(lane == h, top[rows], notes[n])
                    note = jnp.where(lane == TOK_HEADS + h, high, note)
                    notes[n] = jnp.where(lane == 2 * TOK_HEADS + h, total[rows] - high, note)
                parts[n].append(part)
        half = WIDE // 2
        for k, (a, b, d, e), note in zip(places, parts, notes):
            message = [
                a[:, :half], a[:, half:] + b[:, :half], b[:, half:],
                d[:, :half], d[:, half:] + e[:, :half], e[:, half:], note,
            ]
            message = jnp.concatenate(message, axis=1).astype(bf16)
            outbox[pl.ds(2 * k, 2)] = message.reshape(2, TOK_DEV, MESSAGE)
            for n in range(2):

                @pl.when(2 * k + n != c)
                def _():
                    out_copy(2 * k + n).start()

    paired, attended = PAIRED, 0
    for pairs, chunks in SCHEDULE:
        loop(paired, paired + pairs, pair_step)
        attend(attended, chunks)
        paired, attended = paired + pairs, attended + chunks
    inbox[c] = outbox[c]

    def arrived(k):
        s = lax.rem(c + k, COLS)
        out_arrival(s).wait_recv()
        out_copy(s).wait_send()

    loop(1, COLS, arrived)


def main_part(count, starts, feat, token, w_qkv, w_out, w_lift, single, gain, w_tok, pair, w_in, w_pair_out, w_bias):
    def vmem(*shape):
        return pltpu.VMEM(shape, bf16)

    def dma(n):
        return pltpu.SemaphoreType.DMA((n,))

    return pl.pallas_call(
        main_kernel,
        out_shape=[
            jax.ShapeDtypeStruct((TILE_I, TILE_J, C_PAIR), bf16),
            jax.ShapeDtypeStruct((COLS, TOK_DEV, MESSAGE), bf16),
            jax.ShapeDtypeStruct((CAP, C_ATOM), bf16),
            jax.ShapeDtypeStruct((TOK_DEV, C_TOK), f32),
            jax.ShapeDtypeStruct((TOK_DEV, C_TOK), bf16),
        ],
        in_specs=[SMEM] + [HBM] * 13,
        out_specs=[VMEM] * 5,
        scratch_shapes=[
            pltpu.SMEM((CAP // QUERY_BLOCK,), jnp.int32), vmem(CAP, C_ATOM), pltpu.VMEM((1, CAP), jnp.int32),
            vmem(C_ATOM, 3 * C_ATOM), vmem(C_ATOM, C_ATOM), vmem(C_ATOM, C_TOK), vmem(TOK_DEV, C_TOK),
            pltpu.VMEM((C_TOK,), f32), vmem(C_TOK, 4 * C_TOK), vmem(C_PAIR, 2 * HID), vmem(HID, C_PAIR),
            vmem(TOK_HEADS, C_PAIR), dma(12),
            vmem(TILE_I, TILE_J, C_PAIR), dma(CHUNKS),
            vmem(2 * HID + TOK_HEADS, C_PAIR), vmem(C_PAIR + TOK_HEADS, HID),
            pltpu.VMEM((CHUNKS, TOK_HEADS * CHUNK, TILE_J), f32),
            vmem(BEFORE, C_ATOM), vmem(BEFORE, C_ATOM), vmem(AFTER, C_ATOM), dma(2), dma(2),
            vmem(TOK_DEV, C_TOK), vmem(TOK_DEV, 2 * C_TOK),
            vmem(COLS, TOK_DEV, C_TOK), vmem(ROWS, TOK_DEV, 2 * C_TOK),
            dma(COLS), dma(COLS), dma(ROWS), dma(ROWS),
            vmem(COLS, TOK_DEV, MESSAGE), dma(COLS), dma(COLS),
        ],
        compiler_params=pltpu.CompilerParams(
            collective_id=0, has_side_effects=True, vmem_limit_bytes=36 << 20
        ),
        name="main_part",
    )(count, starts, feat, token, w_qkv, w_out, w_lift, single, gain, w_tok, pair, w_in, w_pair_out, w_bias)


def finish_kernel(
    count_ref, pair_ref, inbox, gate_ref, state_ref, mid_ref, token_ref, w_tok_out_ref, w_back_ref,
    token_out_ref, atom_out_ref, pair_out_ref, sem,
):
    write = pltpu.make_async_copy(pair_ref, pair_out_ref, sem)
    write.start()
    block = lax.axis_index("row") * COLS + lax.axis_index("col")
    width = C_TOK // TOK_HEADS
    head = iota((TOK_HEADS, C_TOK), 0) * width
    column = iota((TOK_HEADS, C_TOK), 1)
    head_one = ((column >= head) & (column < head + width)).astype(bf16)
    n = TOK_HEADS
    tails = [inbox[s, :, C_TOK:].astype(f32) for s in range(COLS)]
    tops = [t[:, :n] for t in tails]
    totals = [t[:, n : 2 * n] + t[:, 2 * n : 3 * n] for t in tails]
    top = functools.reduce(jnp.maximum, tops)
    factors = [jnp.exp(t - top) for t in tops]
    total = sum(f * t for f, t in zip(factors, totals))
    factors = jnp.concatenate([f / total for f in factors], axis=0)
    high = factors.astype(bf16)
    low = (factors - high.astype(f32)).astype(bf16)
    factors = dot(high, head_one) + dot(low, head_one)
    mixed = sum(
        factors[s * TOK_DEV : (s + 1) * TOK_DEV] * inbox[s, :, :C_TOK].astype(f32)
        for s in range(COLS)
    )
    gated = (mixed * jax.nn.sigmoid(gate_ref[...].astype(f32))).astype(bf16)
    token_out = (state_ref[...] + dot(gated, w_tok_out_ref[...])).astype(bf16)
    token_out_ref[...] = token_out
    count = count_ref[0]
    member = membership(token_ref[...], count, block).astype(bf16)
    same = (iota((CAP, CAP), 0) == iota((CAP, CAP), 1)).astype(bf16)
    chosen = dot(dot_nt(same, member).astype(bf16), token_out).astype(bf16)
    back = mid_ref[...].astype(f32) + dot(chosen, w_back_ref[...])
    atom_out_ref[...] = jnp.where(iota((CAP, 1), 0) < count, back, 0.0).astype(bf16)
    write.wait()


def finish_part(count, pair, inbox, gate, state, mid, token, w_tok_out, w_back):
    return pl.pallas_call(
        finish_kernel,
        out_shape=[
            jax.ShapeDtypeStruct((TOK_DEV, C_TOK), bf16),
            jax.ShapeDtypeStruct((CAP, C_ATOM), bf16),
            jax.ShapeDtypeStruct(pair.shape, bf16),
        ],
        in_specs=[SMEM, ANY] + [VMEM] * 7,
        out_specs=[VMEM, VMEM, ANY],
        scratch_shapes=[pltpu.SemaphoreType.DMA],
        compiler_params=pltpu.CompilerParams(vmem_limit_bytes=16 << 20),
        name="finish_part",
    )(count, pair, inbox, gate, state, mid, token, w_tok_out, w_back)


def local(
    atom_feat,
    atom_token,
    atom_count,
    window_start,
    w_atom_qkv,
    w_atom_out,
    w_atom_tok,
    single,
    tok_gain,
    w_tok,
    w_tok_out,
    pair,
    w_pair_in,
    w_pair_out,
    w_bias,
    w_back,
):
    token = atom_token.reshape(1, CAP)
    sides = (
        window_start, atom_feat, token, w_atom_qkv, w_atom_out, w_atom_tok, single, tok_gain, w_tok,
        pair, w_pair_in, w_pair_out, w_bias.T,
    )
    sides = [pltpu.with_memory_space_constraint(array, pltpu.HBM) for array in sides]
    pair_new, inbox, mid, state, gate = main_part(atom_count, *sides)
    return tuple(
        finish_part(atom_count, pair_new, inbox, gate, state, mid, token, w_tok_out, w_back)
    )


def solution(mesh):
    tokens = P(("row", "col"), None)
    flat = P(("row", "col"))
    return jax.shard_map(
        local,
        mesh=mesh,
        in_specs=(
            tokens, flat, flat, flat, P(), P(), P(), tokens, P(), P(), P(), P("row", "col", None),
            P(), P(), P(), P(),
        ),
        out_specs=(tokens, tokens, P("row", "col", None)),
        check_vma=False,
    )
```
